128 devices in a mesh: seq: 16 (over z_hi, x, core), head: 8 (over y, z_lo).
Axes of the slice: x: 4, y: 4, z: 4 (z_hi: 2, z_lo: 2; z = z_hi * 2 + z_lo), core: 2. Of those that a mesh axis runs over, the one named last changes fastest.
Arguments:
- hidden: bfloat16 [16384, 2048], P(('seq', 'head')), may hold values from -41 to 41
- w_qkv: bfloat16 [2048, 3072], replicated, may hold values from -0.125 to 0.125
- w_out: bfloat16 [2048, 2048], replicated, may hold values from -0.125 to 0.125
- seg_ids: int32 [16384], replicated, may hold values from 0 to 7, never falling along the last dimension, each value on 1 to 8192 neighbouring positions
- live: int32 [16384], replicated, may hold values 0 or 1
- page_table: int32 [1024], replicated, may hold values from 0 to 1023, as said below
Outputs:
- mixed: bfloat16 [16384, 2048], P(('seq', 'head'))
- kv_pool: bfloat16 [8, 1024, 16, 128], P('head', 'seq')
The draws below stay inside these ranges and needn't reach their ends.
Inputs may be any that keep to these rules, and one draw needn't show every extreme that they name: `page_table`: A permutation of the 1024 pages; pool shard r along seq holds pages r * 64 to (r + 1) * 64 - 1, and the 64 logical pages of each seq group go exactly 4 to each pool shard.
All inputs are finite; a program needn't handle non-finite values.
Results may differ from the reference program's by a relative error of at most 0.0059.
The reference program's roundings to bfloat16 on the way (of `packed`, `weights` and `attended`) count: a program that leaves them out, or rounds other values in their place, can miss the bound.
Values may be sent and summed in bfloat16 or wider, within the bound.
A program may use at most 128 MiB of HBM per device.

```python
import math
import jax
import jax.numpy as jnp
import numpy as np
from jax import lax

D = 2048
H = 32
KVH = 8
HD = 64
PAGE = 16
SEGS = 8
QPK = 4
QKV = 3072
TOKENS = 16384
GT = 1024
MAXLEN = 8192
PAGES = 1024
LP_GROUP = 64
SENDS = 4


def draw_hidden(key, part):
    base = jnp.clip(jax.random.normal(jax.random.fold_in(key, 11), (TOKENS, D), jnp.float32), -6.0, 6.0)
    phase = jax.random.uniform(jax.random.fold_in(key, 15), (), jnp.float32, 0.0, 6.2831853)
    direction = jnp.clip(jax.random.normal(jax.random.fold_in(key, 16), (1, D), jnp.float32), -3.0, 3.0)
    place = jnp.arange(TOKENS, dtype=jnp.float32)[:, None] * (6.2831853 / TOKENS)
    drift = 1.5 * jnp.cos(place + phase) * direction
    sign = jnp.where(jax.random.bernoulli(jax.random.fold_in(key, 17), 0.5, ()), 1.0, -1.0)
    group_of = jnp.arange(TOKENS, dtype=jnp.int32)[:, None] // GT
    alternate = (1 - 2 * (group_of % 2)).astype(jnp.float32)
    drift = drift + 1.5 * sign * alternate * direction
    return jnp.clip(base + drift, -41.0, 41.0).astype(jnp.bfloat16)


def draw_page_table(key, part):
    groups = LP_GROUP // SENDS
    row = jnp.repeat(jnp.arange(groups, dtype=jnp.int32), SENDS)
    dest_keys = jax.random.split(jax.random.fold_in(key, 21), groups)
    dest = jax.vmap(lambda one: jax.random.permutation(one, row))(dest_keys).reshape(PAGES)
    order = jnp.argsort(dest, stable=True)
    sorted_dest = dest[order]
    position = jnp.arange(PAGES, dtype=jnp.int32) % LP_GROUP
    slot_keys = jax.random.split(jax.random.fold_in(key, 22), groups)
    slot_table = jax.vmap(lambda one: jax.random.permutation(one, jnp.arange(LP_GROUP, dtype=jnp.int32)))(slot_keys)
    physical = sorted_dest * LP_GROUP + slot_table[sorted_dest, position]
    return jnp.zeros((PAGES,), jnp.int32).at[order].set(physical.astype(jnp.int32))


def touch_ends(drawn, stream_key, least, high):
    index_at = [jax.random.randint(jax.random.fold_in(stream_key, axis), (), 0, length) for axis, length in enumerate(drawn.shape)]
    longest = drawn.shape.index(max(drawn.shape))
    next_to = index_at[:longest] + [(index_at[longest] + 1) % drawn.shape[longest]] + index_at[longest + 1:]
    return drawn.at[tuple(index_at)].set(least).at[tuple(next_to)].set(high)


def split_up(count, total, most, skew):
    weights = [(1 << 20) // math.isqrt(standing ** skew) + 1 for standing in range(2, count + 1)]
    surplus, given = total - most - (count - 1), [1] * (count - 1)
    while surplus > 0:
        movable = [i for i in range(count - 1) if given[i] < most]
        pool, left = sum([weights[i] for i in movable]), surplus
        for i in movable:
            addition = min(most - given[i], max(1, left * weights[i] // pool), surplus)
            given[i] = given[i] + addition
            surplus = surplus - addition
    return np.array([most] + given)


def ragged_sizes(rng, amount, total, most, slope):
    if amount == 2:
        one = jax.random.randint(rng, (), max(1, total - most), min(most, total - 1) + 1)
        return jnp.stack([one, total - one])
    sizes = jnp.asarray(split_up(amount, total, most, slope), jnp.int32)
    couples = (amount - 1) // 2
    source_of, sink = sizes[1:1 + 2 * couples:2], sizes[2:2 + 2 * couples:2]
    slack = jnp.minimum(source_of - 1, most - sink)
    passed = jax.random.randint(jax.random.fold_in(rng, 1), (couples,), 0, 1 << 20) % (slack + 1)
    sizes = sizes.at[1:1 + 2 * couples:2].set(source_of - passed).at[2:2 + 2 * couples:2].set(sink + passed)
    return sizes[jax.random.permutation(jax.random.fold_in(rng, 2), amount)]


def gaussian(stream_key, shape, width, limit, kind=jnp.bfloat16):
    values = jax.random.normal(stream_key, shape, jnp.float32) * width
    return jnp.minimum(jnp.maximum(values, -limit), limit).astype(kind)


def setup_inputs(seed: int = 0) -> dict:
    key_of = jax.random.split(jax.random.key(seed), 7)
    hidden = draw_hidden(jax.random.fold_in(key_of[6], 71), 0)
    w_qkv = gaussian(key_of[1], (D, QKV), D ** -0.5, 0.125)
    w_out = gaussian(key_of[2], (H * HD, D), (H * HD) ** -0.5, 0.125)
    seg_ids = jnp.searchsorted(jnp.cumsum(ragged_sizes(key_of[3], SEGS, TOKENS, MAXLEN, 0)), jnp.arange(TOKENS), side="right").astype(jnp.int32)
    live = touch_ends((jax.random.randint(key_of[4], (TOKENS,), 0, 16) < 15).astype(jnp.int32), jax.random.fold_in(key_of[4], 1), 0, 1)
    page_table = draw_page_table(jax.random.fold_in(key_of[6], 71), 0)
    return dict(hidden=hidden, w_qkv=w_qkv, w_out=w_out, seg_ids=seg_ids, live=live, page_table=page_table)


def reference(hidden, w_qkv, w_out, seg_ids, live, page_table):
    tokens = hidden.shape[0]
    packed = jnp.dot(hidden, w_qkv, preferred_element_type=jnp.float32).astype(jnp.bfloat16)
    shaped = packed.reshape(tokens, KVH, QPK + 2, HD)
    queries = shaped[:, :, :QPK].astype(jnp.float32)
    keyvals = shaped[:, :, QPK:].reshape(tokens, KVH, 2 * HD)
    keys = keyvals[:, :, :HD].astype(jnp.float32)
    values = keyvals[:, :, HD:].astype(jnp.float32)
    index = jnp.arange(tokens, dtype=jnp.int32)
    block = min(tokens, 512)

    def one_block(number):
        begin = (number * block).astype(jnp.int32)
        q_block = lax.dynamic_slice_in_dim(queries, begin, block, 0)
        q_index = begin + jnp.arange(block, dtype=jnp.int32)
        q_seg = lax.dynamic_slice_in_dim(seg_ids, begin, block, 0)
        allowed = (seg_ids[None, :] == q_seg[:, None]) & (index[None, :] <= q_index[:, None])
        allowed = allowed & ((live[None, :] == 1) | (index[None, :] == q_index[:, None]))

        def one_group(group):
            q_group = lax.dynamic_index_in_dim(q_block, group, 1, keepdims=False)
            k_group = lax.dynamic_index_in_dim(keys, group, 1, keepdims=False)
            v_group = lax.dynamic_index_in_dim(values, group, 1, keepdims=False)
            scores = jnp.einsum("qcd,kd->cqk", q_group, k_group) * 0.015625
            masked = jnp.where(allowed[None], scores, -1e30)
            top = jnp.max(masked, axis=-1, keepdims=True)
            weights = jnp.where(allowed[None], jnp.exp(masked - top), 0.0)
            total = jnp.sum(weights, axis=-1)
            rounded = lax.optimization_barrier(weights.astype(jnp.bfloat16)).astype(jnp.float32)
            return jnp.einsum("cqk,kd->cqd", rounded, v_group) / total[..., None]

        return lax.map(one_group, jnp.arange(KVH, dtype=jnp.int32))

    blocks = lax.map(one_block, jnp.arange(tokens // block, dtype=jnp.int32))
    attended = blocks.transpose(0, 3, 1, 2, 4).reshape(tokens, KVH * QPK * HD).astype(jnp.bfloat16)
    mixed = jnp.dot(attended, w_out, preferred_element_type=jnp.float32).astype(jnp.bfloat16)
    pages = keyvals.reshape(tokens // PAGE, PAGE, KVH, 2 * HD)
    kv_pool = jnp.zeros_like(pages).at[page_table].set(pages)
    return mixed, kv_pool.transpose(2, 0, 1, 3)
```

```python
import functools

import jax
import jax.numpy as jnp
from jax import lax
from jax.experimental import pallas as pl
from jax.experimental.pallas import tpu as pltpu
from jax.sharding import PartitionSpec as P

D = 2048
TOKENS = 16384
KVH = 8
HD = 64
QPK = 4
PAGE = 16
SEQ = 16
ROWS = 128
GT = 1024
COLS = (QPK + 2) * HD
STRIPES = 8
BK = 512
PAD = BK
NEG = -1e30
MESH = pl.DeviceIdType.MESH
bf16, f32 = jnp.bfloat16, jnp.float32


def dealt(s, j):
    slot = (s % 2) * 8 + j
    return jnp.where((s // 2) % 2 == 0, slot, 15 - slot)


def held(s, k):
    slot = s if k % 2 == 0 else 15 - s
    return 2 * k + slot // 8, slot % 8


def project(hid, w, q_out, kv_out, hv, wk, wq, kvs, qs, load, a2a_s, a2a_r, q_s, q_r, g_s, g_r, loc):
    s, j = lax.axis_index("seq"), lax.axis_index("head")
    zh, x, c = s // 8, (s // 2) % 4, s % 2
    to = dealt(s, j)
    mine = to == s

    first = pltpu.make_async_copy(hid, hv, load.at[16])
    first.start()
    loads = []
    for r in range(8):
        g = lax.rem(j + r + 1, 8)
        col = pl.multiple_of(g * COLS + QPK * HD, 128)
        loads.append(pltpu.make_async_copy(w.at[:, pl.ds(col, 2 * HD)], wk.at[r], load.at[r]))
        loads[-1].start()
    for r in range(8):
        g = lax.rem(j + r + 1, 8)
        col = pl.multiple_of(g * COLS, 128)
        loads.append(pltpu.make_async_copy(w.at[:, pl.ds(col, QPK * HD)], wq.at[r], load.at[8 + r]))
        loads[-1].start()

    def block(zz, xx, cc):
        return zz * 8 + xx * 2 + cc

    right, left = lax.rem(x + 1, 4), lax.rem(x + 3, 4)
    far = lax.rem(x + 2, 4)
    peers = [(block(zh, right, c), j), (block(zh, left, c), j), (block(1 - zh, x, c), j), (block(zh, x, 1 - c), j)]

    barrier = pltpu.get_barrier_semaphore()
    for p in peers:
        pl.semaphore_signal(barrier, inc=1, device_id=p, device_id_type=MESH)
    for r in range(7):
        pl.semaphore_signal(barrier, inc=1, device_id=(s, lax.rem(j + r + 1, 8)), device_id_type=MESH)
    for k in range(STRIPES):
        own = mine & (s // 2 == k)

        @pl.when(jnp.logical_not(own))
        def _():
            pl.semaphore_signal(barrier, inc=1, device_id=held(s, k), device_id_type=MESH)

    first.wait()

    row0 = pl.multiple_of(s * GT + j * ROWS, ROWS)
    sends = []
    for r in range(8):
        g = lax.rem(j + r + 1, 8)
        loads[r].wait()
        kvs[r] = jnp.dot(hv[...], wk[r], preferred_element_type=f32).astype(bf16)
        if r == 0:
            pl.semaphore_wait(barrier, jnp.where(mine, 18, 19))

        if r < 7:
            cp = pltpu.make_async_remote_copy(
                src_ref=kvs.at[r],
                dst_ref=kv_out.at[pl.ds(row0, ROWS)],
                send_sem=a2a_s.at[r],
                recv_sem=a2a_r.at[r],
                device_id=(s, g),
                device_id_type=MESH,
            )
            cp.start()
            sends.append(cp)
        else:
            own_kv = pltpu.make_async_copy(kvs.at[r], kv_out.at[pl.ds(row0, ROWS)], loc)
            own_kv.start()

    slot = s // 2
    qsends = []
    for r in range(8):
        g = lax.rem(j + r + 1, 8)
        loads[8 + r].wait()
        qs[r] = (jnp.dot(hv[...], wq[r], preferred_element_type=f32).astype(bf16) * 0.015625).astype(bf16)
        cp = pltpu.make_async_remote_copy(
            src_ref=qs.at[r],
            dst_ref=q_out.at[slot],
            send_sem=q_s.at[r],
            recv_sem=q_r.at[slot],
            device_id=(to, g),
            device_id_type=MESH,
        )
        qsends.append(cp)
        if r < 7:
            cp.start()
        else:

            @pl.when(jnp.logical_not(mine))
            def _():
                cp.start()

            @pl.when(mine)
            def _():
                pltpu.make_async_copy(qs.at[7], q_out.at[slot], q_r.at[slot]).start()

    def rows(b, first_row, count):
        return kv_out.at[pl.ds(pl.multiple_of(b * GT + first_row, 128), count)]

    def arrived(b, first_row, count, i):
        there = rows(b, first_row, count)
        pltpu.make_async_copy(there, there, g_r.at[i]).wait()

    def pass_on(b, first_row, count, i, peer):
        there = rows(b, first_row, count)
        cp = pltpu.make_async_remote_copy(
            src_ref=there,
            dst_ref=there,
            send_sem=g_s.at[i],
            recv_sem=g_r.at[i],
            device_id=peers[peer],
            device_id_type=MESH,
        )
        cp.start()
        sends.append(cp)

    R, L, Z, C = range(4)
    own_kv.wait()
    for r in range(7):
        source = lax.rem(j + 7 - r, 8)
        there = kv_out.at[pl.ds(pl.multiple_of(s * GT + source * ROWS, ROWS), ROWS)]
        pltpu.make_async_copy(there, there, a2a_r.at[r]).wait()
    H = GT // 2
    me = block(zh, x, c)
    pass_on(me, 0, GT, 0, R)
    pass_on(me, 0, GT, 1, L)
    pass_on(me, 0, GT, 2, Z)
    pass_on(me, 0, GT, 3, C)
    bl, br, bf = block(zh, left, c), block(zh, right, c), block(zh, far, c)
    zm, zl, zr, zf = block(1 - zh, x, c), block(1 - zh, left, c), block(1 - zh, right, c), block(1 - zh, far, c)
    arrived(bl, 0, GT, 0)
    pass_on(bl, 0, H, 4, R)
    pass_on(bl, 0, GT, 6, C)
    arrived(br, 0, GT, 1)
    pass_on(br, H, H, 5, L)
    pass_on(br, 0, GT, 7, C)
    arrived(zm, 0, GT, 2)
    pass_on(zm, 0, GT, 10, R)
    pass_on(zm, 0, GT, 11, L)
    pass_on(zm, 0, GT, 12, C)
    arrived(bf, 0, H, 4)
    pass_on(bf, 0, H, 8, C)
    arrived(bf, H, H, 5)
    pass_on(bf, H, H, 9, C)
    arrived(zl, 0, GT, 10)
    pass_on(zl, 0, H, 13, R)
    pass_on(zl, 0, GT, 15, C)
    arrived(zr, 0, GT, 11)
    pass_on(zr, H, H, 14, L)
    pass_on(zr, 0, GT, 16, C)
    arrived(zf, 0, H, 13)
    pass_on(zf, 0, H, 17, C)
    arrived(zf, H, H, 14)
    pass_on(zf, H, H, 18, C)
    d = 1 - c
    arrived(block(zh, x, d), 0, GT, 3)
    arrived(block(zh, left, d), 0, GT, 6)
    arrived(block(zh, right, d), 0, GT, 7)
    arrived(block(zh, far, d), 0, H, 8)
    arrived(block(zh, far, d), H, H, 9)
    arrived(block(1 - zh, x, d), 0, GT, 12)
    arrived(block(1 - zh, left, d), 0, GT, 15)
    arrived(block(1 - zh, right, d), 0, GT, 16)
    arrived(block(1 - zh, far, d), 0, H, 17)
    arrived(block(1 - zh, far, d), H, H, 18)

    for k in range(STRIPES):
        pltpu.make_async_copy(q_out.at[k], q_out.at[k], q_r.at[k]).wait()
    for cp in sends + qsends[:7]:
        cp.wait_send()

    @pl.when(jnp.logical_not(mine))
    def _():
        qsends[7].wait_send()


def attend(count, seg0, inv, code, q, kv_hbm, att, pool, kv, ve, qe, m, acc, sem, page_sem):
    s = lax.axis_index("seq")
    chunk = TOKENS // STRIPES

    def load(k):
        at = pl.multiple_of(k * chunk, chunk)
        return pltpu.make_async_copy(
            kv_hbm.at[pl.ds(at, chunk)], kv.at[pl.ds(pl.multiple_of(PAD + at, 128), chunk)], sem.at[k]
        )

    for k in range(STRIPES):
        load(k).start()

    @pl.loop(0, TOKENS // PAGE // SEQ)
    def _(i):
        at = pl.multiple_of(inv[i] * PAGE, PAGE)
        pltpu.make_async_copy(kv_hbm.at[pl.ds(at, PAGE)], pool.at[pl.ds(pl.multiple_of(i * PAGE, PAGE), PAGE)], page_sem).start()

    kv[:PAD] = jnp.zeros((PAD, 2 * HD), bf16)
    ve[:PAD] = jnp.zeros((PAD, 2 * HD), bf16)
    low = lax.broadcasted_iota(jnp.int32, (1, 2 * HD), 1) < HD
    it = lax.broadcasted_iota(jnp.int32, (ROWS, ROWS), 0)
    iu = lax.broadcasted_iota(jnp.int32, (ROWS, ROWS), 1)

    def scores(c, keys):
        return lax.dot_general(qe[c], keys, (((1,), (1,)), ((), ())), preferred_element_type=f32)

    @pl.loop(0, STRIPES)
    def _(k):
        load(k).wait()

        @pl.loop(0, chunk // 256)
        def _(i):
            at = pl.ds(pl.multiple_of(PAD + k * chunk + i * 256, 256), 256)
            ve[at] = jnp.where(low, jnp.ones((256, 2 * HD), bf16), kv[at])

        slot = jnp.where(k % 2 == 0, s, 15 - s)
        stripe = 16 * k + slot
        t0 = stripe * ROWS
        own = seg0[k]
        zero = jnp.zeros((ROWS, HD), bf16)
        for c in range(QPK):
            qe[c] = jnp.concatenate([q[k, :, c * HD : (c + 1) * HD], zero], axis=1)

        here = pl.ds(pl.multiple_of(PAD + t0, 128), ROWS)
        cu = jnp.broadcast_to(code[pl.ds(PAD // 128 + stripe, 1), :], (ROWS, ROWS))
        ct = cu.T
        allowed = ((cu & 15) == (ct & 15)) & (iu <= it) & ((cu < 16) | (iu == it))
        same = (ct[:, :1] & 15) == own
        for c in range(QPK):
            sc = jnp.where(allowed, scores(c, kv[here]), NEG)
            top = jnp.max(sc, axis=1, keepdims=True)
            p = jnp.exp(sc - top)
            acc[c] = jnp.dot(p.astype(bf16), ve[here], preferred_element_type=f32)
            m[c] = jnp.where(same, top, -NEG)

        @pl.loop(0, count[k])
        def _(i):
            first = PAD + t0 - (i + 1) * BK
            at = pl.ds(pl.multiple_of(first, 128), BK)
            bias = [
                jnp.where(code[pl.ds(first // 128 + n, 1), :] == own, 0.0, NEG) for n in range(BK // 128)
            ]
            bias = jnp.concatenate(bias, axis=1)
            for c in range(QPK):
                sc = scores(c, kv[at]) + bias
                old = m[c]
                top = jnp.maximum(old, jnp.max(sc, axis=1, keepdims=True))
                p = jnp.exp(sc - top)
                acc[c] = acc[c] * jnp.exp(old - top) + jnp.dot(p.astype(bf16), ve[at], preferred_element_type=f32)
                m[c] = top

        for c in range(0, QPK, 2):
            a, b = acc[c], acc[c + 1]
            first_head = pltpu.roll(a, HD, 1) / a
            second_head = b / pltpu.roll(b, HD, 1)
            att[k, :, c * HD : (c + 2) * HD] = jnp.where(low, first_head, second_head).astype(bf16)

    pltpu.make_async_copy(kv_hbm.at[pl.ds(0, GT)], pool, page_sem).wait()


def mix(att, w, out, wv, got, acc, load, a_s, a_r):
    s, j = lax.axis_index("seq"), lax.axis_index("head")
    to = dealt(s, j)
    mine = to == s
    loads = []
    for r in range(8):
        h = lax.rem(j + 8 - r, 8)
        at = pl.multiple_of(h * QPK * HD, QPK * HD)
        loads.append(pltpu.make_async_copy(w.at[pl.ds(at, QPK * HD)], wv.at[r], load.at[r]))
        loads[-1].start()

    barrier = pltpu.get_barrier_semaphore()
    for r in range(8):
        h = lax.rem(j + r + 1, 8)
        if r < 7:
            pl.semaphore_signal(barrier, inc=1, device_id=(to, h), device_id_type=MESH)
        else:

            @pl.when(jnp.logical_not(mine))
            def _():
                pl.semaphore_signal(barrier, inc=1, device_id=(to, h), device_id_type=MESH)

    pl.semaphore_wait(barrier, jnp.where(mine, 7, 8))

    copies = []
    for k in range(STRIPES):
        own = mine & (s // 2 == k)
        cp = pltpu.make_async_remote_copy(
            src_ref=att.at[k],
            dst_ref=got.at[j],
            send_sem=a_s.at[k],
            recv_sem=a_r.at[j],
            device_id=held(s, k),
            device_id_type=MESH,
        )
        copies.append((own, cp))

        @pl.when(jnp.logical_not(own))
        def _():
            cp.start()

        @pl.when(own)
        def _():
            pltpu.make_async_copy(att.at[k], got.at[j], a_r.at[j]).start()

    for r in range(8):
        h = lax.rem(j + 8 - r, 8)
        loads[r].wait()
        pltpu.make_async_copy(got.at[h], got.at[h], a_r.at[h]).wait()
        part = jnp.dot(got[h], wv[r], preferred_element_type=f32)
        if r == 0:
            acc[...] = part
        elif r < 7:
            acc[...] += part
        else:
            out[...] = (acc[...] + part).astype(bf16)
    for own, cp in copies:

        @pl.when(jnp.logical_not(own))
        def _():
            cp.wait_send()


ANY = pl.BlockSpec(memory_space=pl.ANY)
SMEM = pl.BlockSpec(memory_space=pltpu.SMEM)
VMEM = pl.BlockSpec(memory_space=pltpu.VMEM)
DMA = pltpu.SemaphoreType.DMA


def shards(hidden, w_qkv, w_out, seg_ids, live, page_table):
    s = lax.axis_index("seq")
    q, kv = pl.pallas_call(
        project,
        out_shape=(
            jax.ShapeDtypeStruct((STRIPES, ROWS, QPK * HD), bf16),
            jax.ShapeDtypeStruct((TOKENS, 2 * HD), bf16),
        ),
        in_specs=[ANY, ANY],
        out_specs=(ANY, ANY),
        scratch_shapes=[
            pltpu.VMEM((ROWS, D), bf16),
            pltpu.VMEM((KVH, D, 2 * HD), bf16),
            pltpu.VMEM((KVH, D, QPK * HD), bf16),
            pltpu.VMEM((KVH, ROWS, 2 * HD), bf16),
            pltpu.VMEM((KVH, ROWS, QPK * HD), bf16),
            DMA((17,)),
            DMA((7,)),
            DMA((7,)),
            DMA((8,)),
            DMA((8,)),
            DMA((19,)),
            DMA((19,)),
            DMA,
        ],
        compiler_params=pltpu.CompilerParams(collective_id=0, has_side_effects=True, vmem_limit_bytes=40 << 20),
        name="project",
    )(hidden, w_qkv)

    heads = seg_ids.reshape(STRIPES, SEQ, ROWS)[:, :, 0]
    even = lax.dynamic_slice_in_dim(heads, s, 1, 1)[:, 0]
    odd = lax.dynamic_slice_in_dim(heads, 15 - s, 1, 1)[:, 0]
    number = jnp.arange(STRIPES, dtype=jnp.int32)
    is_even = number % 2 == 0
    seg0 = jnp.where(is_even, even, odd)
    begin = jnp.sum((seg_ids[None, :] < seg0[:, None]).astype(jnp.int32), axis=1)
    t0 = (16 * number + jnp.where(is_even, s, 15 - s)) * ROWS
    count = (t0 - begin + BK - 1) // BK
    page = s * (TOKENS // PAGE // SEQ) + jnp.arange(TOKENS // PAGE // SEQ, dtype=jnp.int32)
    inv = jnp.sum(
        jnp.where(page_table[None, :] == page[:, None], jnp.arange(TOKENS // PAGE, dtype=jnp.int32)[None, :], 0), axis=1
    )
    code = (seg_ids + 16 * (1 - live)).reshape(TOKENS // 128, 128)
    code = jnp.concatenate([jnp.full((PAD // 128, 128), 255, jnp.int32), code], axis=0)

    att, pool = pl.pallas_call(
        attend,
        out_shape=(
            jax.ShapeDtypeStruct((STRIPES, ROWS, QPK * HD), bf16),
            jax.ShapeDtypeStruct((GT, 2 * HD), bf16),
        ),
        in_specs=[SMEM, SMEM, SMEM, VMEM, VMEM, ANY],
        out_specs=(VMEM, ANY),
        scratch_shapes=[
            pltpu.VMEM((PAD + TOKENS, 2 * HD), bf16),
            pltpu.VMEM((PAD + TOKENS, 2 * HD), bf16),
            pltpu.VMEM((QPK, ROWS, 2 * HD), bf16),
            pltpu.VMEM((QPK, ROWS, 1), f32),
            pltpu.VMEM((QPK, ROWS, 2 * HD), f32),
            DMA((STRIPES,)),
            DMA,
        ],
        compiler_params=pltpu.CompilerParams(vmem_limit_bytes=40 << 20),
        name="attend",
    )(count, seg0, inv, code, q, kv)

    mixed = pl.pallas_call(
        mix,
        out_shape=jax.ShapeDtypeStruct((ROWS, D), bf16),
        in_specs=[ANY, ANY],
        out_specs=VMEM,
        scratch_shapes=[
            pltpu.VMEM((KVH, QPK * HD, D), bf16),
            pltpu.VMEM((KVH, ROWS, QPK * HD), bf16),
            pltpu.VMEM((ROWS, D), f32),
            DMA((8,)),
            DMA((8,)),
            DMA((8,)),
        ],
        compiler_params=pltpu.CompilerParams(collective_id=1, has_side_effects=True, vmem_limit_bytes=40 << 20),
        name="mix",
    )(att, w_out)
    return mixed, pool.reshape(1, TOKENS // PAGE // SEQ, PAGE, 2 * HD)


def solution(mesh):
    placed = (P(("seq", "head"), None), P(), P(), P(), P(), P())
    return jax.shard_map(
        shards,
        mesh=mesh,
        in_specs=placed,
        out_specs=(P(("seq", "head"), None), P("head", "seq", None, None)),
        check_vma=False,
    )
```

```python
import functools

import jax
import jax.numpy as jnp
from jax import lax
from jax.experimental import pallas as pl
from jax.experimental.pallas import tpu as pltpu
from jax.sharding import PartitionSpec as P

D = 2048
TOKENS = 16384
KVH = 8
HD = 64
QPK = 4
PAGE = 16
SEQ = 16
SEGS = 8
ROWS = 128
GT = 1024
COLS = (QPK + 2) * HD
STRIPES = 8
BK = 512
PAD = 3 * BK
NEG = -1e30
MESH = pl.DeviceIdType.MESH
bf16, f32 = jnp.bfloat16, jnp.float32


def dealt(s, j):
    slot = (s % 2) * 8 + j
    return jnp.where((s // 2) % 2 == 0, slot, 15 - slot)


def held(s, k):
    slot = s if k % 2 == 0 else 15 - s
    return 2 * k + slot // 8, slot % 8


def project(hid, w, q_out, kv_out, hv, wk, wq, kvs, qs, load, a2a_s, a2a_r, q_s, q_r, g_s, g_r, loc):
    s, j = lax.axis_index("seq"), lax.axis_index("head")
    zh, x, c = s // 8, (s // 2) % 4, s % 2
    to = dealt(s, j)
    mine = to == s

    first = pltpu.make_async_copy(hid, hv, load.at[16])
    first.start()
    loads = []
    for r in range(8):
        g = lax.rem(j + r + 1, 8)
        col = pl.multiple_of(g * COLS + QPK * HD, 128)
        loads.append(pltpu.make_async_copy(w.at[:, pl.ds(col, 2 * HD)], wk.at[r], load.at[r]))
        loads[-1].start()
    for r in range(8):
        g = lax.rem(j + r + 1, 8)
        col = pl.multiple_of(g * COLS, 128)
        loads.append(pltpu.make_async_copy(w.at[:, pl.ds(col, QPK * HD)], wq.at[r], load.at[8 + r]))
        loads[-1].start()

    def block(zz, xx, cc):
        return zz * 8 + xx * 2 + cc

    right, left = lax.rem(x + 1, 4), lax.rem(x + 3, 4)
    far = lax.rem(x + 2, 4)
    peers = [(block(zh, right, c), j), (block(zh, left, c), j), (block(1 - zh, x, c), j), (block(zh, x, 1 - c), j)]

    barrier = pltpu.get_barrier_semaphore()
    for p in peers:
        pl.semaphore_signal(barrier, inc=1, device_id=p, device_id_type=MESH)
    for r in range(7):
        pl.semaphore_signal(barrier, inc=1, device_id=(s, lax.rem(j + r + 1, 8)), device_id_type=MESH)
    for k in range(STRIPES):
        own = mine & (s // 2 == k)

        @pl.when(jnp.logical_not(own))
        def _():
            pl.semaphore_signal(barrier, inc=1, device_id=held(s, k), device_id_type=MESH)

    first.wait()

    row0 = pl.multiple_of(s * GT + j * ROWS, ROWS)
    sends = []
    for r in range(8):
        g = lax.rem(j + r + 1, 8)
        loads[r].wait()
        kvs[r] = jnp.dot(hv[...], wk[r], preferred_element_type=f32).astype(bf16)
        if r == 0:
            pl.semaphore_wait(barrier, jnp.where(mine, 18, 19))

        if r < 7:
            cp = pltpu.make_async_remote_copy(
                src_ref=kvs.at[r],
                dst_ref=kv_out.at[pl.ds(row0, ROWS)],
                send_sem=a2a_s.at[r],
                recv_sem=a2a_r.at[r],
                device_id=(s, g),
                device_id_type=MESH,
            )
            cp.start()
            sends.append(cp)
        else:
            own_kv = pltpu.make_async_copy(kvs.at[r], kv_out.at[pl.ds(row0, ROWS)], loc)
            own_kv.start()

    slot = s // 2
    qsends = []
    for r in range(8):
        g = lax.rem(j + r + 1, 8)
        loads[8 + r].wait()
        qs[r] = (jnp.dot(hv[...], wq[r], preferred_element_type=f32).astype(bf16) * 0.015625).astype(bf16)
        cp = pltpu.make_async_remote_copy(
            src_ref=qs.at[r],
            dst_ref=q_out.at[slot],
            send_sem=q_s.at[r],
            recv_sem=q_r.at[slot],
            device_id=(to, g),
            device_id_type=MESH,
        )
        qsends.append(cp)
        if r < 7:
            cp.start()
        else:

            @pl.when(jnp.logical_not(mine))
            def _():
                cp.start()

            @pl.when(mine)
            def _():
                pltpu.make_async_copy(qs.at[7], q_out.at[slot], q_r.at[slot]).start()

    def rows(b, first_row, count):
        return kv_out.at[pl.ds(pl.multiple_of(b * GT + first_row, 128), count)]

    def arrived(b, first_row, count, i):
        there = rows(b, first_row, count)
        pltpu.make_async_copy(there, there, g_r.at[i]).wait()

    def pass_on(b, first_row, count, i, peer):
        there = rows(b, first_row, count)
        cp = pltpu.make_async_remote_copy(
            src_ref=there,
            dst_ref=there,
            send_sem=g_s.at[i],
            recv_sem=g_r.at[i],
            device_id=peers[peer],
            device_id_type=MESH,
        )
        cp.start()
        sends.append(cp)

    R, L, Z, C = range(4)
    own_kv.wait()
    for r in range(7):
        source = lax.rem(j + 7 - r, 8)
        there = kv_out.at[pl.ds(pl.multiple_of(s * GT + source * ROWS, ROWS), ROWS)]
        pltpu.make_async_copy(there, there, a2a_r.at[r]).wait()
    H = GT // 2
    me = block(zh, x, c)
    pass_on(me, 0, GT, 0, R)
    pass_on(me, 0, GT, 1, L)
    pass_on(me, 0, GT, 2, Z)
    pass_on(me, 0, GT, 3, C)
    bl, br, bf = block(zh, left, c), block(zh, right, c), block(zh, far, c)
    zm, zl, zr, zf = block(1 - zh, x, c), block(1 - zh, left, c), block(1 - zh, right, c), block(1 - zh, far, c)
    arrived(bl, 0, GT, 0)
    pass_on(bl, 0, H, 4, R)
    pass_on(bl, 0, GT, 6, C)
    arrived(br, 0, GT, 1)
    pass_on(br, H, H, 5, L)
    pass_on(br, 0, GT, 7, C)
    arrived(zm, 0, GT, 2)
    pass_on(zm, 0, GT, 10, R)
    pass_on(zm, 0, GT, 11, L)
    pass_on(zm, 0, GT, 12, C)
    arrived(bf, 0, H, 4)
    pass_on(bf, 0, H, 8, C)
    arrived(bf, H, H, 5)
    pass_on(bf, H, H, 9, C)
    arrived(zl, 0, GT, 10)
    pass_on(zl, 0, H, 13, R)
    pass_on(zl, 0, GT, 15, C)
    arrived(zr, 0, GT, 11)
    pass_on(zr, H, H, 14, L)
    pass_on(zr, 0, GT, 16, C)
    arrived(zf, 0, H, 13)
    pass_on(zf, 0, H, 17, C)
    arrived(zf, H, H, 14)
    pass_on(zf, H, H, 18, C)
    d = 1 - c
    arrived(block(zh, x, d), 0, GT, 3)
    arrived(block(zh, left, d), 0, GT, 6)
    arrived(block(zh, right, d), 0, GT, 7)
    arrived(block(zh, far, d), 0, H, 8)
    arrived(block(zh, far, d), H, H, 9)
    arrived(block(1 - zh, x, d), 0, GT, 12)
    arrived(block(1 - zh, left, d), 0, GT, 15)
    arrived(block(1 - zh, right, d), 0, GT, 16)
    arrived(block(1 - zh, far, d), 0, H, 17)
    arrived(block(1 - zh, far, d), H, H, 18)

    for k in range(STRIPES):
        pltpu.make_async_copy(q_out.at[k], q_out.at[k], q_r.at[k]).wait()
    for cp in sends + qsends[:7]:
        cp.wait_send()

    @pl.when(jnp.logical_not(mine))
    def _():
        qsends[7].wait_send()


NT = (((1,), (1,)), ((), ()))
VR = HD + 16


def attend(count, seg0, inv, code, q, kv_hbm, att, pool, kv, kx, vt, qt, m, acc, sa, sb, sem, page_sem):
    s = lax.axis_index("seq")
    chunk = TOKENS // STRIPES

    def load(k):
        at = pl.multiple_of(k * chunk, chunk)
        return pltpu.make_async_copy(kv_hbm.at[pl.ds(at, chunk)], kv.at[pl.ds(at, chunk)], sem.at[k])

    for k in range(STRIPES):
        load(k).start()

    @pl.loop(0, TOKENS // PAGE // SEQ)
    def _(i):
        at = pl.multiple_of(inv[i] * PAGE, PAGE)
        to = pl.multiple_of(i * PAGE, PAGE)
        pltpu.make_async_copy(kv_hbm.at[pl.ds(at, PAGE)], pool.at[pl.ds(to, PAGE)], page_sem).start()

    down = lax.broadcasted_iota(jnp.int32, (128, 128), 0)
    along = lax.broadcasted_iota(jnp.int32, (128, 128), 1)
    eye = (down == along).astype(bf16)
    pick = (along[:HD] == down[:HD] + HD).astype(bf16)
    low = along < HD
    marks = (down >= HD) & (down < HD + SEGS)
    mark_row = (along[:1] >= HD) & (along[:1] < HD + SEGS)
    kx[:PAD] = jnp.broadcast_to(jnp.where(mark_row, NEG, 0.0), (PAD, 2 * HD)).astype(bf16)
    vt[:HD, :PAD] = jnp.zeros((HD, PAD), bf16)
    vt[HD:, :] = jnp.ones((VR - HD, PAD + TOKENS), bf16)

    def peak(sc):
        return jnp.max(sc.reshape(sc.shape[0] // 8, 8, sc.shape[1]), axis=0)

    def scores(first):
        keys = kx[pl.ds(pl.multiple_of(first, 128), BK), :]
        return jnp.dot(keys, qt[...], preferred_element_type=f32)

    @pl.loop(0, STRIPES)
    def _(k):
        load(k).wait()
        at = pl.multiple_of(k * chunk, chunk)
        rows = kv[pl.ds(at, chunk), :]
        vt[:HD, pl.ds(pl.multiple_of(PAD + at, 128), chunk)] = lax.dot_general(
            pick, rows, NT, preferred_element_type=f32
        ).astype(bf16)
        for n in range(chunk // 128):
            row = code[pl.ds(k * (chunk // 128) + n, 1), :]
            mark = jnp.where(marks & (row != down - HD), NEG, 0.0).astype(bf16)
            mark = lax.dot_general(eye, mark, NT, preferred_element_type=f32).astype(bf16)
            to = pl.multiple_of(PAD + at + n * 128, 128)
            kx[pl.ds(to, 128), :] = jnp.where(low, rows[n * 128 : (n + 1) * 128], mark)

        stripe = 16 * k + jnp.where(k % 2 == 0, s, 15 - s)
        own = seg0[k]
        here = pl.multiple_of(PAD + stripe * ROWS, 128)
        for c in range(0, QPK, 2):
            t = q[k, :, c * HD : (c + 2) * HD].T
            qt[:HD, c * ROWS : (c + 1) * ROWS] = t[:HD]
            qt[:HD, (c + 1) * ROWS : (c + 2) * ROWS] = t[HD:]
        qt[HD:, :] = (lax.broadcasted_iota(jnp.int32, (HD, QPK * ROWS), 0) == own).astype(bf16)

        sc = scores(here - BK)
        sa[...] = sc
        near = peak(sc)

        row = code[pl.ds(stripe, 1), :]
        ct = jnp.broadcast_to(row, (ROWS, ROWS))
        cu = ct.T
        allowed = ((cu & 15) == (ct & 15)) & (down <= along) & ((cu < 16) | (down == along))
        same = (row & 15) == own
        sc = jnp.dot(kx[pl.ds(here, ROWS), :HD], qt[:HD, :], preferred_element_type=f32)
        sc = jnp.concatenate(
            [jnp.where(allowed, sc[:, c * ROWS : (c + 1) * ROWS], NEG) for c in range(QPK)], axis=1
        )
        top = jnp.max(peak(sc), axis=0, keepdims=True)
        p = jnp.exp(sc - top).astype(bf16)
        acc[...] = jnp.dot(vt[:, pl.ds(here, ROWS)], p, preferred_element_type=f32)
        m[...] = jnp.where(jnp.concatenate([same] * QPK, axis=1), top, -NEG)

        def half(b, src, dst, peaks):
            first = here - (b + 1) * BK
            old = m[...]
            top = jnp.maximum(old, jnp.max(peaks, axis=0, keepdims=True))
            m[...] = top
            sc = scores(first - BK)
            dst[...] = sc
            p = jnp.exp(src[...] - top).astype(bf16)
            part = jnp.dot(vt[:, pl.ds(pl.multiple_of(first, 128), BK)], p, preferred_element_type=f32)
            acc[...] = acc[...] * jnp.exp(old - top) + part
            return peak(sc)

        def pair(i, peaks):
            peaks = half(2 * i, sa, sb, peaks)
            return half(2 * i + 1, sb, sa, peaks)

        lax.fori_loop(0, (count[k] + 1) // 2, pair, near)
        for c in range(0, QPK, 2):
            one, two = slice(c * ROWS, (c + 1) * ROWS), slice((c + 1) * ROWS, (c + 2) * ROWS)
            done = jnp.concatenate(
                [acc[:HD, one] / acc[HD : HD + 1, one], acc[:HD, two] / acc[HD : HD + 1, two]], axis=0
            )
            att[k, :, c * HD : (c + 2) * HD] = done.T.astype(bf16)

    pltpu.make_async_copy(kv_hbm.at[pl.ds(0, GT)], pool, page_sem).wait()


def mix(att, w, out, wv, got, acc, load, a_s, a_r):
    s, j = lax.axis_index("seq"), lax.axis_index("head")
    to = dealt(s, j)
    mine = to == s
    loads = []
    for r in range(8):
        h = lax.rem(j + 8 - r, 8)
        at = pl.multiple_of(h * QPK * HD, QPK * HD)
        loads.append(pltpu.make_async_copy(w.at[pl.ds(at, QPK * HD)], wv.at[r], load.at[r]))
        loads[-1].start()

    barrier = pltpu.get_barrier_semaphore()
    for r in range(8):
        h = lax.rem(j + r + 1, 8)
        if r < 7:
            pl.semaphore_signal(barrier, inc=1, device_id=(to, h), device_id_type=MESH)
        else:

            @pl.when(jnp.logical_not(mine))
            def _():
                pl.semaphore_signal(barrier, inc=1, device_id=(to, h), device_id_type=MESH)

    pl.semaphore_wait(barrier, jnp.where(mine, 7, 8))

    copies = []
    for k in range(STRIPES):
        own = mine & (s // 2 == k)
        cp = pltpu.make_async_remote_copy(
            src_ref=att.at[k],
            dst_ref=got.at[j],
            send_sem=a_s.at[k],
            recv_sem=a_r.at[j],
            device_id=held(s, k),
            device_id_type=MESH,
        )
        copies.append((own, cp))

        @pl.when(jnp.logical_not(own))
        def _():
            cp.start()

        @pl.when(own)
        def _():
            pltpu.make_async_copy(att.at[k], got.at[j], a_r.at[j]).start()

    for r in range(8):
        h = lax.rem(j + 8 - r, 8)
        loads[r].wait()
        pltpu.make_async_copy(got.at[h], got.at[h], a_r.at[h]).wait()
        part = jnp.dot(got[h], wv[r], preferred_element_type=f32)
        if r == 0:
            acc[...] = part
        elif r < 7:
            acc[...] += part
        else:
            out[...] = (acc[...] + part).astype(bf16)
    for own, cp in copies:

        @pl.when(jnp.logical_not(own))
        def _():
            cp.wait_send()


ANY = pl.BlockSpec(memory_space=pl.ANY)
SMEM = pl.BlockSpec(memory_space=pltpu.SMEM)
VMEM = pl.BlockSpec(memory_space=pltpu.VMEM)
DMA = pltpu.SemaphoreType.DMA


def shards(hidden, w_qkv, w_out, seg_ids, live, page_table):
    s = lax.axis_index("seq")
    q, kv = pl.pallas_call(
        project,
        out_shape=(
            jax.ShapeDtypeStruct((STRIPES, ROWS, QPK * HD), bf16),
            jax.ShapeDtypeStruct((TOKENS, 2 * HD), bf16),
        ),
        in_specs=[ANY, ANY],
        out_specs=(ANY, ANY),
        scratch_shapes=[
            pltpu.VMEM((ROWS, D), bf16),
            pltpu.VMEM((KVH, D, 2 * HD), bf16),
            pltpu.VMEM((KVH, D, QPK * HD), bf16),
            pltpu.VMEM((KVH, ROWS, 2 * HD), bf16),
            pltpu.VMEM((KVH, ROWS, QPK * HD), bf16),
            DMA((17,)),
            DMA((7,)),
            DMA((7,)),
            DMA((8,)),
            DMA((8,)),
            DMA((19,)),
            DMA((19,)),
            DMA,
        ],
        compiler_params=pltpu.CompilerParams(collective_id=0, has_side_effects=True, vmem_limit_bytes=40 << 20),
        name="project",
    )(hidden, w_qkv)

    heads = seg_ids.reshape(STRIPES, SEQ, ROWS)[:, :, 0]
    even = lax.dynamic_slice_in_dim(heads, s, 1, 1)[:, 0]
    odd = lax.dynamic_slice_in_dim(heads, 15 - s, 1, 1)[:, 0]
    number = jnp.arange(STRIPES, dtype=jnp.int32)
    is_even = number % 2 == 0
    seg0 = jnp.where(is_even, even, odd)
    begin = jnp.sum((seg_ids[None, :] < seg0[:, None]).astype(jnp.int32), axis=1)
    t0 = (16 * number + jnp.where(is_even, s, 15 - s)) * ROWS
    count = (t0 - begin + BK - 1) // BK
    page = s * (TOKENS // PAGE // SEQ) + jnp.arange(TOKENS // PAGE // SEQ, dtype=jnp.int32)
    inv = jnp.sum(
        jnp.where(page_table[None, :] == page[:, None], jnp.arange(TOKENS // PAGE, dtype=jnp.int32)[None, :], 0), axis=1
    )
    code = (seg_ids + 16 * (1 - live)).reshape(TOKENS // 128, 128)

    att, pool = pl.pallas_call(
        attend,
        out_shape=(
            jax.ShapeDtypeStruct((STRIPES, ROWS, QPK * HD), bf16),
            jax.ShapeDtypeStruct((GT, 2 * HD), bf16),
        ),
        in_specs=[SMEM, SMEM, SMEM, VMEM, VMEM, ANY],
        out_specs=(VMEM, ANY),
        scratch_shapes=[
            pltpu.VMEM((TOKENS, 2 * HD), bf16),
            pltpu.VMEM((PAD + TOKENS, 2 * HD), bf16),
            pltpu.VMEM((VR, PAD + TOKENS), bf16),
            pltpu.VMEM((2 * HD, QPK * ROWS), bf16),
            pltpu.VMEM((1, QPK * ROWS), f32),
            pltpu.VMEM((VR, QPK * ROWS), f32),
            pltpu.VMEM((BK, QPK * ROWS), f32),
            pltpu.VMEM((BK, QPK * ROWS), f32),
            DMA((STRIPES,)),
            DMA,
        ],
        compiler_params=pltpu.CompilerParams(vmem_limit_bytes=40 << 20),
        name="attend",
    )(count, seg0, inv, code, q, kv)

    mixed = pl.pallas_call(
        mix,
        out_shape=jax.ShapeDtypeStruct((ROWS, D), bf16),
        in_specs=[ANY, ANY],
        out_specs=VMEM,
        scratch_shapes=[
            pltpu.VMEM((KVH, QPK * HD, D), bf16),
            pltpu.VMEM((KVH, ROWS, QPK * HD), bf16),
            pltpu.VMEM((ROWS, D), f32),
            DMA((8,)),
            DMA((8,)),
            DMA((8,)),
        ],
        compiler_params=pltpu.CompilerParams(collective_id=1, has_side_effects=True, vmem_limit_bytes=40 << 20),
        name="mix",
    )(att, w_out)
    return mixed, pool.reshape(1, TOKENS // PAGE // SEQ, PAGE, 2 * HD)


def solution(mesh):
    placed = (P(("seq", "head"), None), P(), P(), P(), P(), P())
    return jax.shard_map(
        shards,
        mesh=mesh,
        in_specs=placed,
        out_specs=(P(("seq", "head"), None), P("head", "seq", None, None)),
        check_vma=False,
    )
```

```python
import functools

import jax
import jax.numpy as jnp
from jax import lax
from jax.experimental import pallas as pl
from jax.experimental.pallas import tpu as pltpu
from jax.sharding import PartitionSpec as P

D = 2048
TOKENS = 16384
KVH = 8
HD = 64
QPK = 4
PAGE = 16
SEQ = 16
SEGS = 8
ROWS = 128
GT = 1024
COLS = (QPK + 2) * HD
STRIPES = 8
BK = 512
PAD = 3 * BK
EARLY = 3
NEG = -1e30
MESH = pl.DeviceIdType.MESH
bf16, f32 = jnp.bfloat16, jnp.float32


MASKS = (0, 11, 13, 6)


def flip(value, x):
    if isinstance(x, int):
        bits = [(MASKS[x] >> n) % 2 for n in range(4)]
    else:
        low, high = x % 2, x // 2
        both = (low + high) % 2
        bits = [both, low, high, both]
    return sum(((value // (1 << n) + bits[n]) % 2) * (1 << n) for n in range(4))


def dealt(s, j):
    return flip((s % 2) * 8 + j, (s // 2) % 4)


def held(s, k):
    slot = flip(s, k % 4)
    return 2 * k + slot // 8, slot % 8


def project(hid, w, q_out, kv_out, hv, wk, wq, kvs, qs, load, a2a_s, a2a_r, q_s, q_r, g_s, g_r, loc):
    s, j = lax.axis_index("seq"), lax.axis_index("head")
    zh, x, c = s // 8, (s // 2) % 4, s % 2
    to = dealt(s, j)
    mine = to == s

    first = pltpu.make_async_copy(hid, hv, load.at[16])
    first.start()
    loads = []
    for r in range(8):
        g = lax.rem(j + r + 1, 8)
        col = pl.multiple_of(g * COLS + QPK * HD, 128)
        loads.append(pltpu.make_async_copy(w.at[:, pl.ds(col, 2 * HD)], wk.at[r], load.at[r]))
        loads[-1].start()
    for r in range(8):
        g = lax.rem(j + r + 1, 8)
        col = pl.multiple_of(g * COLS, 128)
        loads.append(pltpu.make_async_copy(w.at[:, pl.ds(col, QPK * HD)], wq.at[r], load.at[8 + r]))
        loads[-1].start()

    def block(zz, xx, cc):
        return zz * 8 + xx * 2 + cc

    right, left = lax.rem(x + 1, 4), lax.rem(x + 3, 4)
    far = lax.rem(x + 2, 4)
    peers = [(block(zh, right, c), j), (block(zh, left, c), j), (block(1 - zh, x, c), j), (block(zh, x, 1 - c), j)]

    barrier = pltpu.get_barrier_semaphore()
    for p in peers:
        pl.semaphore_signal(barrier, inc=1, device_id=p, device_id_type=MESH)
    for r in range(7):
        pl.semaphore_signal(barrier, inc=1, device_id=(s, lax.rem(j + r + 1, 8)), device_id_type=MESH)
    for k in range(STRIPES):
        own = mine & (s // 2 == k)

        @pl.when(jnp.logical_not(own))
        def _():
            pl.semaphore_signal(barrier, inc=1, device_id=held(s, k), device_id_type=MESH)

    first.wait()

    row0 = pl.multiple_of(s * GT + j * ROWS, ROWS)
    sends = []
    for r in range(8):
        g = lax.rem(j + r + 1, 8)
        loads[r].wait()
        kvs[r] = jnp.dot(hv[...], wk[r], preferred_element_type=f32).astype(bf16)
        if r == 0:
            pl.semaphore_wait(barrier, jnp.where(mine, 18, 19))
        if r < 7:
            cp = pltpu.make_async_remote_copy(
                src_ref=kvs.at[r],
                dst_ref=kv_out.at[pl.ds(row0, ROWS)],
                send_sem=a2a_s.at[r],
                recv_sem=a2a_r.at[r],
                device_id=(s, g),
                device_id_type=MESH,
            )
            cp.start()
            sends.append(cp)
        else:
            own_kv = pltpu.make_async_copy(kvs.at[r], kv_out.at[pl.ds(row0, ROWS)], loc)
            own_kv.start()

    H = GT // 2
    R, L, Z, C = range(4)

    def half(b, h):
        return kv_out.at[pl.ds(pl.multiple_of(b * GT + h * H, 128), H)]

    count = [0]

    def pass_on(b, h, *to_peers):
        for peer in to_peers:
            i = count[0]
            count[0] += 1
            cp = pltpu.make_async_remote_copy(
                src_ref=half(b, h),
                dst_ref=half(b, h),
                send_sem=g_s.at[i],
                recv_sem=g_r.at[i],
                device_id=peers[peer],
                device_id_type=MESH,
            )
            cp.start()
            sends.append(cp)

    def arrived(b, h, i):
        pltpu.make_async_copy(half(b, h), half(b, h), g_r.at[i]).wait()

    slot = s // 2
    qsends = []

    def query(r):
        loads[8 + r].wait()
        qs[r] = (jnp.dot(hv[...], wq[r], preferred_element_type=f32).astype(bf16) * 0.015625).astype(bf16)

    def send_query(r):
        cp = pltpu.make_async_remote_copy(
            src_ref=qs.at[r],
            dst_ref=q_out.at[slot],
            send_sem=q_s.at[r],
            recv_sem=q_r.at[slot],
            device_id=(to, lax.rem(j + r + 1, 8)),
            device_id_type=MESH,
        )
        qsends.append(cp)
        if r < 7:
            cp.start()
        else:

            @pl.when(jnp.logical_not(mine))
            def _():
                cp.start()

            @pl.when(mine)
            def _():
                pltpu.make_async_copy(qs.at[7], q_out.at[slot], q_r.at[slot]).start()

    for r in range(EARLY):
        query(r)
    own_kv.wait()
    for r in range(7):
        source = lax.rem(j + 7 - r, 8)
        there = kv_out.at[pl.ds(pl.multiple_of(s * GT + source * ROWS, ROWS), ROWS)]
        pltpu.make_async_copy(there, there, a2a_r.at[r]).wait()
    me = block(zh, x, c)
    bl, br, bf = block(zh, left, c), block(zh, right, c), block(zh, far, c)
    zm, zl, zr, zf = block(1 - zh, x, c), block(1 - zh, left, c), block(1 - zh, right, c), block(1 - zh, far, c)
    pass_on(me, 0, R, Z)
    pass_on(me, 1, L, Z)
    pass_on(me, 1, R)
    pass_on(me, 0, L, C)
    pass_on(me, 1, C)
    for r in range(EARLY, 8):
        query(r)
    for r in range(8):
        send_query(r)
    arrived(bl, 0, 0)
    pass_on(bl, 0, R, C)
    arrived(br, 1, 2)
    pass_on(br, 1, L, C)
    arrived(zm, 0, 1)
    pass_on(zm, 0, R, L, C)
    arrived(zm, 1, 3)
    pass_on(zm, 1, R, L, C)
    arrived(bl, 1, 4)
    pass_on(bl, 1, C)
    arrived(br, 0, 5)
    pass_on(br, 0, C)
    arrived(bf, 0, 8)
    pass_on(bf, 0, Z, C)
    arrived(bf, 1, 10)
    pass_on(bf, 1, Z, C)
    arrived(zl, 0, 12)
    pass_on(zl, 0, C)
    arrived(zr, 0, 13)
    pass_on(zr, 0, C)
    arrived(zl, 1, 15)
    pass_on(zl, 1, C)
    arrived(zr, 1, 16)
    pass_on(zr, 1, C)
    arrived(zf, 0, 20)
    pass_on(zf, 0, C)
    arrived(zf, 1, 22)
    pass_on(zf, 1, C)
    d = 1 - c
    for zz, xx, first, second in (
        (zh, x, 6, 7),
        (zh, left, 9, 18),
        (zh, right, 19, 11),
        (zh, far, 21, 23),
        (1 - zh, x, 14, 17),
        (1 - zh, left, 24, 26),
        (1 - zh, right, 25, 27),
        (1 - zh, far, 28, 29),
    ):
        arrived(block(zz, xx, d), 0, first)
        arrived(block(zz, xx, d), 1, second)

    for k in range(STRIPES):
        pltpu.make_async_copy(q_out.at[k], q_out.at[k], q_r.at[k]).wait()
    for cp in sends + qsends[:7]:
        cp.wait_send()

    @pl.when(jnp.logical_not(mine))
    def _():
        qsends[7].wait_send()


NT = (((1,), (1,)), ((), ()))
VR = HD + 16


def attend(count, seg0, inv, code, q, kv_hbm, att, pool, kv, kx, vt, qt, m, acc, sa, sb, sem, page_sem):
    s = lax.axis_index("seq")
    chunk = TOKENS // STRIPES

    def load(k):
        at = pl.multiple_of(k * chunk, chunk)
        return pltpu.make_async_copy(kv_hbm.at[pl.ds(at, chunk)], kv.at[pl.ds(at, chunk)], sem.at[k])

    for k in range(STRIPES):
        load(k).start()

    @pl.loop(0, TOKENS // PAGE // SEQ)
    def _(i):
        at = pl.multiple_of(inv[i] * PAGE, PAGE)
        to = pl.multiple_of(i * PAGE, PAGE)
        pltpu.make_async_copy(kv_hbm.at[pl.ds(at, PAGE)], pool.at[pl.ds(to, PAGE)], page_sem).start()

    down = lax.broadcasted_iota(jnp.int32, (128, 128), 0)
    along = lax.broadcasted_iota(jnp.int32, (128, 128), 1)
    eye = (down == along).astype(bf16)
    pick = (along[:HD] == down[:HD] + HD).astype(bf16)
    low = along < HD
    marks = (down >= HD) & (down < HD + SEGS)
    mark_row = (along[:1] >= HD) & (along[:1] < HD + SEGS)
    kx[:PAD] = jnp.broadcast_to(jnp.where(mark_row, NEG, 0.0), (PAD, 2 * HD)).astype(bf16)
    vt[:HD, :PAD] = jnp.zeros((HD, PAD), bf16)
    vt[HD:, :] = jnp.ones((VR - HD, PAD + TOKENS), bf16)

    def peak(sc):
        return jnp.max(sc.reshape(sc.shape[0] // 8, 8, sc.shape[1]), axis=0)

    def scores(first):
        keys = kx[pl.ds(pl.multiple_of(first, 128), BK), :]
        return jnp.dot(keys, qt[...], preferred_element_type=f32)

    @pl.loop(0, STRIPES)
    def _(k):
        load(k).wait()
        at = pl.multiple_of(k * chunk, chunk)
        rows = kv[pl.ds(at, chunk), :]
        vt[:HD, pl.ds(pl.multiple_of(PAD + at, 128), chunk)] = lax.dot_general(
            pick, rows, NT, preferred_element_type=f32
        ).astype(bf16)
        for n in range(chunk // 128):
            row = code[pl.ds(k * (chunk // 128) + n, 1), :]
            mark = jnp.where(marks & (row != down - HD), NEG, 0.0).astype(bf16)
            mark = lax.dot_general(eye, mark, NT, preferred_element_type=f32).astype(bf16)
            to = pl.multiple_of(PAD + at + n * 128, 128)
            kx[pl.ds(to, 128), :] = jnp.where(low, rows[n * 128 : (n + 1) * 128], mark)

        stripe = 16 * k + flip(s, k % 4)
        own = seg0[k]
        here = pl.multiple_of(PAD + stripe * ROWS, 128)
        for c in range(0, QPK, 2):
            t = q[k, :, c * HD : (c + 2) * HD].T
            qt[:HD, c * ROWS : (c + 1) * ROWS] = t[:HD]
            qt[:HD, (c + 1) * ROWS : (c + 2) * ROWS] = t[HD:]
        qt[HD:, :] = (lax.broadcasted_iota(jnp.int32, (HD, QPK * ROWS), 0) == own).astype(bf16)

        sc = scores(here - BK)
        sa[...] = sc
        near = peak(sc)

        row = code[pl.ds(stripe, 1), :]
        ct = jnp.broadcast_to(row, (ROWS, ROWS))
        cu = ct.T
        allowed = ((cu & 15) == (ct & 15)) & (down <= along) & ((cu < 16) | (down == along))
        same = (row & 15) == own
        sc = jnp.dot(kx[pl.ds(here, ROWS), :HD], qt[:HD, :], preferred_element_type=f32)
        sc = jnp.concatenate(
            [jnp.where(allowed, sc[:, c * ROWS : (c + 1) * ROWS], NEG) for c in range(QPK)], axis=1
        )
        top = jnp.max(peak(sc), axis=0, keepdims=True)
        p = jnp.exp(sc - top).astype(bf16)
        acc[...] = jnp.dot(vt[:, pl.ds(here, ROWS)], p, preferred_element_type=f32)
        m[...] = jnp.where(jnp.concatenate([same] * QPK, axis=1), top, -NEG)

        def half(b, src, dst, peaks):
            first = here - (b + 1) * BK
            old = m[...]
            top = jnp.maximum(old, jnp.max(peaks, axis=0, keepdims=True))
            m[...] = top
            sc = scores(first - BK)
            dst[...] = sc
            p = jnp.exp(src[...] - top).astype(bf16)
            part = jnp.dot(vt[:, pl.ds(pl.multiple_of(first, 128), BK)], p, preferred_element_type=f32)
            acc[...] = acc[...] * jnp.exp(old - top) + part
            return peak(sc)

        def pair(i, peaks):
            peaks = half(2 * i, sa, sb, peaks)
            return half(2 * i + 1, sb, sa, peaks)

        lax.fori_loop(0, (count[k] + 1) // 2, pair, near)
        for c in range(0, QPK, 2):
            one, two = slice(c * ROWS, (c + 1) * ROWS), slice((c + 1) * ROWS, (c + 2) * ROWS)
            done = jnp.concatenate(
                [acc[:HD, one] / acc[HD : HD + 1, one], acc[:HD, two] / acc[HD : HD + 1, two]], axis=0
            )
            att[k, :, c * HD : (c + 2) * HD] = done.T.astype(bf16)

    pltpu.make_async_copy(kv_hbm.at[pl.ds(0, GT)], pool, page_sem).wait()


def mix(att, w, out, wv, got, acc, load, a_s, a_r):
    s, j = lax.axis_index("seq"), lax.axis_index("head")
    to = dealt(s, j)
    mine = to == s
    loads = []
    for r in range(8):
        h = lax.rem(j + 8 - r, 8)
        at = pl.multiple_of(h * QPK * HD, QPK * HD)
        loads.append(pltpu.make_async_copy(w.at[pl.ds(at, QPK * HD)], wv.at[r], load.at[r]))
        loads[-1].start()

    barrier = pltpu.get_barrier_semaphore()
    for r in range(8):
        h = lax.rem(j + r + 1, 8)
        if r < 7:
            pl.semaphore_signal(barrier, inc=1, device_id=(to, h), device_id_type=MESH)
        else:

            @pl.when(jnp.logical_not(mine))
            def _():
                pl.semaphore_signal(barrier, inc=1, device_id=(to, h), device_id_type=MESH)

    pl.semaphore_wait(barrier, jnp.where(mine, 7, 8))

    copies = []
    for k in range(STRIPES):
        own = mine & (s // 2 == k)
        cp = pltpu.make_async_remote_copy(
            src_ref=att.at[k],
            dst_ref=got.at[j],
            send_sem=a_s.at[k],
            recv_sem=a_r.at[j],
            device_id=held(s, k),
            device_id_type=MESH,
        )
        copies.append((own, cp))

        @pl.when(jnp.logical_not(own))
        def _():
            cp.start()

        @pl.when(own)
        def _():
            pltpu.make_async_copy(att.at[k], got.at[j], a_r.at[j]).start()

    for r in range(8):
        h = lax.rem(j + 8 - r, 8)
        loads[r].wait()
        pltpu.make_async_copy(got.at[h], got.at[h], a_r.at[h]).wait()
        part = jnp.dot(got[h], wv[r], preferred_element_type=f32)
        if r == 0:
            acc[...] = part
        elif r < 7:
            acc[...] += part
        else:
            out[...] = (acc[...] + part).astype(bf16)
    for own, cp in copies:

        @pl.when(jnp.logical_not(own))
        def _():
            cp.wait_send()


ANY = pl.BlockSpec(memory_space=pl.ANY)
SMEM = pl.BlockSpec(memory_space=pltpu.SMEM)
VMEM = pl.BlockSpec(memory_space=pltpu.VMEM)
DMA = pltpu.SemaphoreType.DMA


def shards(hidden, w_qkv, w_out, seg_ids, live, page_table):
    s = lax.axis_index("seq")
    q, kv = pl.pallas_call(
        project,
        out_shape=(
            jax.ShapeDtypeStruct((STRIPES, ROWS, QPK * HD), bf16),
            jax.ShapeDtypeStruct((TOKENS, 2 * HD), bf16),
        ),
        in_specs=[ANY, ANY],
        out_specs=(ANY, ANY),
        scratch_shapes=[
            pltpu.VMEM((ROWS, D), bf16),
            pltpu.VMEM((KVH, D, 2 * HD), bf16),
            pltpu.VMEM((KVH, D, QPK * HD), bf16),
            pltpu.VMEM((KVH, ROWS, 2 * HD), bf16),
            pltpu.VMEM((KVH, ROWS, QPK * HD), bf16),
            DMA((17,)),
            DMA((7,)),
            DMA((7,)),
            DMA((8,)),
            DMA((8,)),
            DMA((30,)),
            DMA((30,)),
            DMA,
        ],
        compiler_params=pltpu.CompilerParams(collective_id=0, has_side_effects=True, vmem_limit_bytes=40 << 20),
        name="project",
    )(hidden, w_qkv)

    heads = seg_ids.reshape(STRIPES, SEQ, ROWS)[:, :, 0]
    number = jnp.arange(STRIPES, dtype=jnp.int32)
    slots = flip(s, number % 4)
    seg0 = jnp.sum(jnp.where(jnp.arange(SEQ, dtype=jnp.int32)[None, :] == slots[:, None], heads, 0), axis=1)
    begin = jnp.sum((seg_ids[None, :] < seg0[:, None]).astype(jnp.int32), axis=1)
    t0 = (16 * number + slots) * ROWS
    count = (t0 - begin + BK - 1) // BK
    page = s * (TOKENS // PAGE // SEQ) + jnp.arange(TOKENS // PAGE // SEQ, dtype=jnp.int32)
    inv = jnp.sum(
        jnp.where(page_table[None, :] == page[:, None], jnp.arange(TOKENS // PAGE, dtype=jnp.int32)[None, :], 0), axis=1
    )
    code = (seg_ids + 16 * (1 - live)).reshape(TOKENS // 128, 128)

    att, pool = pl.pallas_call(
        attend,
        out_shape=(
            jax.ShapeDtypeStruct((STRIPES, ROWS, QPK * HD), bf16),
            jax.ShapeDtypeStruct((GT, 2 * HD), bf16),
        ),
        in_specs=[SMEM, SMEM, SMEM, VMEM, VMEM, ANY],
        out_specs=(VMEM, ANY),
        scratch_shapes=[
            pltpu.VMEM((TOKENS, 2 * HD), bf16),
            pltpu.VMEM((PAD + TOKENS, 2 * HD), bf16),
            pltpu.VMEM((VR, PAD + TOKENS), bf16),
            pltpu.VMEM((2 * HD, QPK * ROWS), bf16),
            pltpu.VMEM((1, QPK * ROWS), f32),
            pltpu.VMEM((VR, QPK * ROWS), f32),
            pltpu.VMEM((BK, QPK * ROWS), f32),
            pltpu.VMEM((BK, QPK * ROWS), f32),
            DMA((STRIPES,)),
            DMA,
        ],
        compiler_params=pltpu.CompilerParams(vmem_limit_bytes=40 << 20),
        name="attend",
    )(count, seg0, inv, code, q, kv)

    mixed = pl.pallas_call(
        mix,
        out_shape=jax.ShapeDtypeStruct((ROWS, D), bf16),
        in_specs=[ANY, ANY],
        out_specs=VMEM,
        scratch_shapes=[
            pltpu.VMEM((KVH, QPK * HD, D), bf16),
            pltpu.VMEM((KVH, ROWS, QPK * HD), bf16),
            pltpu.VMEM((ROWS, D), f32),
            DMA((8,)),
            DMA((8,)),
            DMA((8,)),
        ],
        compiler_params=pltpu.CompilerParams(collective_id=1, has_side_effects=True, vmem_limit_bytes=40 << 20),
        name="mix",
    )(att, w_out)
    return mixed, pool.reshape(1, TOKENS // PAGE // SEQ, PAGE, 2 * HD)


def solution(mesh):
    placed = (P(("seq", "head"), None), P(), P(), P(), P(), P())
    return jax.shard_map(
        shards,
        mesh=mesh,
        in_specs=placed,
        out_specs=(P(("seq", "head"), None), P("head", "seq", None, None)),
        check_vma=False,
    )
```

```python
import functools

import jax
import jax.numpy as jnp
from jax import lax
from jax.experimental import pallas as pl
from jax.experimental.pallas import tpu as pltpu
from jax.sharding import PartitionSpec as P

D = 2048
TOKENS = 16384
KVH = 8
HD = 64
QPK = 4
PAGE = 16
SEQ = 16
SEGS = 8
ROWS = 128
GT = 1024
COLS = (QPK + 2) * HD
STRIPES = 8
BK = 512
PAD = 2 * BK
META = STRIPES + 64
EARLY = 3
NEG = -1e30
MESH = pl.DeviceIdType.MESH
bf16, f32 = jnp.bfloat16, jnp.float32


MASKS = (0, 11, 13, 6)


NT = (((1,), (1,)), ((), ()))
VR = HD + 16


def flip(value, x):
    if isinstance(x, int):
        bits = [(MASKS[x] >> n) % 2 for n in range(4)]
    else:
        low, high = x % 2, x // 2
        both = (low + high) % 2
        bits = [both, low, high, both]
    return sum(((value // (1 << n) + bits[n]) % 2) * (1 << n) for n in range(4))


def dealt(s, j):
    return flip((s % 2) * 8 + j, (s // 2) % 4)


def held(s, k):
    slot = flip(s, k % 4)
    return 2 * k + slot // 8, slot % 8


def project(
    hv, w, seg, live, table, q_out, kv_out, kx, vt, code, meta,
    wk, wq, kvs, qs, load, a2a_s, a2a_r, q_s, q_r, g_s, g_r, loc,
):
    s, j = lax.axis_index("seq"), lax.axis_index("head")
    zh, x, c = s // 8, (s // 2) % 4, s % 2
    to = dealt(s, j)
    mine = to == s

    loads = []
    for r in range(8):
        g = lax.rem(j + r + 1, 8)
        col = pl.multiple_of(g * COLS + QPK * HD, 128)
        loads.append(pltpu.make_async_copy(w.at[:, pl.ds(col, 2 * HD)], wk.at[r], load.at[r]))
        loads[-1].start()
    for r in range(8):
        g = lax.rem(j + r + 1, 8)
        col = pl.multiple_of(g * COLS, 128)
        loads.append(pltpu.make_async_copy(w.at[:, pl.ds(col, QPK * HD)], wq.at[r], load.at[8 + r]))

    def block(zz, xx, cc):
        return zz * 8 + xx * 2 + cc

    right, left = lax.rem(x + 1, 4), lax.rem(x + 3, 4)
    far = lax.rem(x + 2, 4)
    peers = [(block(zh, right, c), j), (block(zh, left, c), j), (block(1 - zh, x, c), j), (block(zh, x, 1 - c), j)]

    barrier = pltpu.get_barrier_semaphore()
    for p in peers:
        pl.semaphore_signal(barrier, inc=1, device_id=p, device_id_type=MESH)
    for r in range(7):
        pl.semaphore_signal(barrier, inc=1, device_id=(s, lax.rem(j + r + 1, 8)), device_id_type=MESH)
    for k in range(STRIPES):
        own = mine & (s // 2 == k)

        @pl.when(jnp.logical_not(own))
        def _():
            pl.semaphore_signal(barrier, inc=1, device_id=held(s, k), device_id_type=MESH)

    down = lax.broadcasted_iota(jnp.int32, (128, 128), 0)
    along = lax.broadcasted_iota(jnp.int32, (128, 128), 1)
    eye = (down == along).astype(bf16)
    pick = (along[:HD] == down[:HD] + HD).astype(bf16)
    marks = (down >= HD) & (down < HD + SEGS)
    mark_row = (along[:1] >= HD) & (along[:1] < HD + SEGS)

    def tables():
        code[...] = seg[...] + 16 * (1 - live[...])
        lane = along[:1]
        for k in range(STRIPES):
            stripe = 16 * k + flip(s, k % 4)
            own = seg[pl.ds(stripe, 1), :][:, :1]
            before = jnp.where(seg[...] < own, 1.0, 0.0)
            begin = jnp.sum(jnp.sum(before, axis=0, keepdims=True), axis=1, keepdims=True).astype(jnp.int32)
            blocks = lax.shift_right_logical(stripe * ROWS - begin + BK - 1, BK.bit_length() - 1)
            meta[k : k + 1, :] = jnp.where(lane == 0, blocks, own)
        at = jnp.zeros((64, 128), f32)
        for n in range(TOKENS // PAGE // 128):
            hit = table[n : n + 1, :] == 64 * s + down[:64]
            at += jnp.where(hit, (n * 128 + along[:64]).astype(f32), 0.0)
        logical = jnp.sum(at, axis=1, keepdims=True).astype(jnp.int32)
        meta[STRIPES:, :] = jnp.broadcast_to(logical, (64, 128))
        kx[:PAD] = jnp.broadcast_to(jnp.where(mark_row, NEG, 0.0), (PAD, 2 * HD)).astype(bf16)
        vt[:HD, :PAD] = jnp.zeros((HD, PAD), bf16)
        vt[HD:, :] = jnp.ones((VR - HD, PAD + TOKENS), bf16)

    def mark_keys(first, stop):
        @pl.loop(first, stop)
        def _(i):
            for n in range(8):
                row = code[pl.ds(i * 8 + n, 1), :]
                mark = jnp.where(marks & (row != down - HD), NEG, 0.0).astype(bf16)
                mark = lax.dot_general(eye, mark, NT, preferred_element_type=f32).astype(bf16)
                kx[pl.ds(pl.multiple_of(PAD + (i * 8 + n) * 128, 128), 128), :] = mark

    def use(b, h):
        at = pl.multiple_of(b * GT + h * (GT // 2), 128)
        to = pl.multiple_of(PAD + at, 128)
        rows = kv_out[pl.ds(at, GT // 2), :]
        vt[:HD, pl.ds(to, GT // 2)] = lax.dot_general(pick, rows, NT, preferred_element_type=f32).astype(bf16)
        kx[pl.ds(to, GT // 2), :] = jnp.where(along[:1] < HD, rows, kx[pl.ds(to, GT // 2), :])

    row0 = pl.multiple_of(s * GT + j * ROWS, ROWS)
    sends = []
    for r in range(8):
        g = lax.rem(j + r + 1, 8)
        loads[r].wait()
        kvs[r] = jnp.dot(hv[...], wk[r], preferred_element_type=f32).astype(bf16)
        if r == 0:
            pl.semaphore_wait(barrier, jnp.where(mine, 18, 19))
        if r < 7:
            cp = pltpu.make_async_remote_copy(
                src_ref=kvs.at[r],
                dst_ref=kv_out.at[pl.ds(row0, ROWS)],
                send_sem=a2a_s.at[r],
                recv_sem=a2a_r.at[r],
                device_id=(s, g),
                device_id_type=MESH,
            )
            cp.start()
            sends.append(cp)
        else:
            own_kv = pltpu.make_async_copy(kvs.at[r], kv_out.at[pl.ds(row0, ROWS)], loc)
            own_kv.start()

    H = GT // 2
    R, L, Z, C = range(4)

    def half(b, h):
        return kv_out.at[pl.ds(pl.multiple_of(b * GT + h * H, 128), H)]

    count = [0]

    def pass_on(b, h, *to_peers):
        for peer in to_peers:
            i = count[0]
            count[0] += 1
            cp = pltpu.make_async_remote_copy(
                src_ref=half(b, h),
                dst_ref=half(b, h),
                send_sem=g_s.at[i],
                recv_sem=g_r.at[i],
                device_id=peers[peer],
                device_id_type=MESH,
            )
            cp.start()
            sends.append(cp)

    def arrived(b, h, i):
        pltpu.make_async_copy(half(b, h), half(b, h), g_r.at[i]).wait()

    slot = s // 2
    qsends = []

    def query(r):
        loads[8 + r].wait()
        qs[r] = (jnp.dot(hv[...], wq[r], preferred_element_type=f32).astype(bf16) * 0.015625).astype(bf16)

    def send_query(r):
        cp = pltpu.make_async_remote_copy(
            src_ref=qs.at[r],
            dst_ref=q_out.at[slot],
            send_sem=q_s.at[r],
            recv_sem=q_r.at[slot],
            device_id=(to, lax.rem(j + r + 1, 8)),
            device_id_type=MESH,
        )
        qsends.append(cp)
        if r < 7:
            cp.start()
        else:

            @pl.when(jnp.logical_not(mine))
            def _():
                cp.start()

            @pl.when(mine)
            def _():
                pltpu.make_async_copy(qs.at[7], q_out.at[slot], q_r.at[slot]).start()

    for r in range(8):
        loads[8 + r].start()
    tables()
    mark_keys(0, 8)
    for r in range(EARLY):
        query(r)
    own_kv.wait()
    for r in range(7):
        source = lax.rem(j + 7 - r, 8)
        there = kv_out.at[pl.ds(pl.multiple_of(s * GT + source * ROWS, ROWS), ROWS)]
        pltpu.make_async_copy(there, there, a2a_r.at[r]).wait()
    me = block(zh, x, c)
    bl, br, bf = block(zh, left, c), block(zh, right, c), block(zh, far, c)
    zm, zl, zr, zf = block(1 - zh, x, c), block(1 - zh, left, c), block(1 - zh, right, c), block(1 - zh, far, c)
    pass_on(me, 0, R, Z)
    pass_on(me, 1, L, Z)
    pass_on(me, 1, R)
    pass_on(me, 0, L, C)
    pass_on(me, 1, C)
    for r in range(EARLY, 8):
        query(r)
    for r in range(8):
        send_query(r)
    mark_keys(8, 16)
    d = 1 - c
    ome, ol, or_, of = block(zh, x, d), block(zh, left, d), block(zh, right, d), block(zh, far, d)
    oz, ozl, ozr, ozf = block(1 - zh, x, d), block(1 - zh, left, d), block(1 - zh, right, d), block(1 - zh, far, d)
    arrived(bl, 0, 0)
    pass_on(bl, 0, R, C)
    arrived(br, 1, 2)
    pass_on(br, 1, L, C)
    arrived(zm, 0, 1)
    pass_on(zm, 0, R, L, C)
    use(me, 0)
    use(me, 1)
    arrived(zm, 1, 3)
    pass_on(zm, 1, R, L, C)
    arrived(bl, 1, 4)
    pass_on(bl, 1, C)
    arrived(br, 0, 5)
    pass_on(br, 0, C)
    use(bl, 0)
    use(br, 1)
    arrived(bf, 0, 8)
    pass_on(bf, 0, Z, C)
    arrived(bf, 1, 10)
    pass_on(bf, 1, Z, C)

    def other(b, h, i):
        arrived(b, h, i)
        use(b, h)

    use(zm, 0)
    use(zm, 1)
    use(bl, 1)
    use(br, 0)
    other(ome, 0, 6)
    other(ome, 1, 7)
    other(ol, 0, 9)
    other(or_, 1, 11)
    other(oz, 0, 14)
    arrived(zl, 0, 12)
    pass_on(zl, 0, C)
    arrived(zr, 0, 13)
    pass_on(zr, 0, C)
    other(oz, 1, 17)
    other(ol, 1, 18)
    other(or_, 0, 19)
    use(bf, 0)
    use(bf, 1)
    other(of, 0, 21)
    other(of, 1, 23)
    arrived(zf, 0, 20)
    pass_on(zf, 0, C)
    use(zl, 0)
    use(zr, 0)
    arrived(zl, 1, 15)
    pass_on(zl, 1, C)
    arrived(zr, 1, 16)
    pass_on(zr, 1, C)
    arrived(zf, 1, 22)
    pass_on(zf, 1, C)
    use(zf, 0)
    other(ozl, 0, 24)
    other(ozr, 0, 25)
    use(zl, 1)
    use(zr, 1)
    other(ozf, 0, 26)
    use(zf, 1)
    other(ozl, 1, 27)
    other(ozr, 1, 28)
    other(ozf, 1, 29)

    for k in range(STRIPES):
        pltpu.make_async_copy(q_out.at[k], q_out.at[k], q_r.at[k]).wait()
    for cp in sends + qsends[:7]:
        cp.wait_send()

    @pl.when(jnp.logical_not(mine))
    def _():
        qsends[7].wait_send()


def attend(meta_in, code, q, kv, kx, vt, att, pool, meta, qt, m, acc, sa, sb, sem, page_sem):
    s = lax.axis_index("seq")
    fetch = pltpu.make_async_copy(meta_in, meta, sem)
    fetch.start()
    down = lax.broadcasted_iota(jnp.int32, (128, 128), 0)
    along = lax.broadcasted_iota(jnp.int32, (128, 128), 1)

    def peak(sc):
        return jnp.max(sc.reshape(sc.shape[0] // 8, 8, sc.shape[1]), axis=0)

    def scores(first):
        keys = kx[pl.ds(pl.multiple_of(first, 128), BK), :]
        return jnp.dot(keys, qt[...], preferred_element_type=f32)

    fetch.wait()

    @pl.loop(0, TOKENS // PAGE // SEQ)
    def _(i):
        at = pl.multiple_of(meta[STRIPES + i, 0] * PAGE, PAGE)
        to = pl.multiple_of(i * PAGE, PAGE)
        pltpu.make_async_copy(kv.at[pl.ds(at, PAGE)], pool.at[pl.ds(to, PAGE)], page_sem).start()

    @pl.loop(0, STRIPES)
    def _(k):
        stripe = 16 * k + flip(s, k % 4)
        own = meta[k, 1]
        here = pl.multiple_of(PAD + stripe * ROWS, 128)
        for c in range(0, QPK, 2):
            t = q[k, :, c * HD : (c + 2) * HD].T
            qt[:HD, c * ROWS : (c + 1) * ROWS] = t[:HD]
            qt[:HD, (c + 1) * ROWS : (c + 2) * ROWS] = t[HD:]
        qt[HD:, :] = (lax.broadcasted_iota(jnp.int32, (HD, QPK * ROWS), 0) == own).astype(bf16)

        sc = scores(here - BK)
        sa[...] = sc
        near = peak(sc)

        row = code[pl.ds(stripe, 1), :]
        ct = jnp.broadcast_to(row, (ROWS, ROWS))
        cu = ct.T
        allowed = ((cu & 15) == (ct & 15)) & (down <= along) & ((cu < 16) | (down == along))
        same = (row & 15) == own
        sc = jnp.dot(kx[pl.ds(here, ROWS), :HD], qt[:HD, :], preferred_element_type=f32)
        sc = jnp.concatenate(
            [jnp.where(allowed, sc[:, c * ROWS : (c + 1) * ROWS], NEG) for c in range(QPK)], axis=1
        )
        top = jnp.max(peak(sc), axis=0, keepdims=True)
        p = jnp.exp(sc - top).astype(bf16)
        acc[...] = jnp.dot(vt[:, pl.ds(here, ROWS)], p, preferred_element_type=f32)
        m[...] = jnp.where(jnp.concatenate([same] * QPK, axis=1), top, -NEG)

        def weigh(b, src, peaks, dst=None):
            first = here - (b + 1) * BK
            old = m[...]
            top = jnp.maximum(old, jnp.max(peaks, axis=0, keepdims=True))
            m[...] = top
            if dst is not None:
                sc = scores(first - BK)
                dst[...] = sc
            p = jnp.exp(src[...] - top).astype(bf16)
            part = jnp.dot(vt[:, pl.ds(pl.multiple_of(first, 128), BK)], p, preferred_element_type=f32)
            acc[...] = acc[...] * jnp.exp(old - top) + part
            return None if dst is None else peak(sc)

        def pair(i, peaks):
            peaks = weigh(2 * i, sa, peaks, sb)
            return weigh(2 * i + 1, sb, peaks, sa)

        blocks = meta[k, 0]
        last = lax.fori_loop(0, blocks // 2, pair, near)

        @pl.when(blocks % 2 == 1)
        def _():
            weigh(blocks - 1, sa, last)

        for c in range(0, QPK, 2):
            one, two = slice(c * ROWS, (c + 1) * ROWS), slice((c + 1) * ROWS, (c + 2) * ROWS)
            done = jnp.concatenate(
                [acc[:HD, one] / acc[HD : HD + 1, one], acc[:HD, two] / acc[HD : HD + 1, two]], axis=0
            )
            att[k, :, c * HD : (c + 2) * HD] = done.T.astype(bf16)

    pltpu.make_async_copy(kv.at[pl.ds(0, GT)], pool, page_sem).wait()


def mix(att, w, out, got, acc, a_s, a_r):
    s, j = lax.axis_index("seq"), lax.axis_index("head")
    to = dealt(s, j)
    mine = to == s
    barrier = pltpu.get_barrier_semaphore()
    for r in range(8):
        h = lax.rem(j + r + 1, 8)
        if r < 7:
            pl.semaphore_signal(barrier, inc=1, device_id=(to, h), device_id_type=MESH)
        else:

            @pl.when(jnp.logical_not(mine))
            def _():
                pl.semaphore_signal(barrier, inc=1, device_id=(to, h), device_id_type=MESH)

    pl.semaphore_wait(barrier, jnp.where(mine, 7, 8))

    copies = []
    for k in range(STRIPES):
        own = mine & (s // 2 == k)
        cp = pltpu.make_async_remote_copy(
            src_ref=att.at[k],
            dst_ref=got.at[j],
            send_sem=a_s.at[k],
            recv_sem=a_r.at[j],
            device_id=held(s, k),
            device_id_type=MESH,
        )
        copies.append((own, cp))

        @pl.when(jnp.logical_not(own))
        def _():
            cp.start()

        @pl.when(own)
        def _():
            pltpu.make_async_copy(att.at[k], got.at[j], a_r.at[j]).start()

    for r in range(8):
        h = lax.rem(j + 8 - r, 8)
        pltpu.make_async_copy(got.at[h], got.at[h], a_r.at[h]).wait()
        part = jnp.dot(
            got[h], w[pl.ds(pl.multiple_of(h * QPK * HD, QPK * HD), QPK * HD), :], preferred_element_type=f32
        )
        if r == 0:
            acc[...] = part
        elif r < 7:
            acc[...] += part
        else:
            out[...] = (acc[...] + part).astype(bf16)
    for own, cp in copies:

        @pl.when(jnp.logical_not(own))
        def _():
            cp.wait_send()


ANY = pl.BlockSpec(memory_space=pl.ANY)
SMEM = pl.BlockSpec(memory_space=pltpu.SMEM)
VMEM = pl.BlockSpec(memory_space=pltpu.VMEM)
DMA = pltpu.SemaphoreType.DMA


HBM = pl.BlockSpec(memory_space=pltpu.HBM)


def shards(hidden, w_qkv, w_out, seg_ids, live, page_table):
    q, kv, kx, vt, code, meta = pl.pallas_call(
        project,
        out_shape=(
            jax.ShapeDtypeStruct((STRIPES, ROWS, QPK * HD), bf16),
            jax.ShapeDtypeStruct((TOKENS, 2 * HD), bf16),
            jax.ShapeDtypeStruct((PAD + TOKENS, 2 * HD), bf16),
            jax.ShapeDtypeStruct((VR, PAD + TOKENS), bf16),
            jax.ShapeDtypeStruct((TOKENS // 128, 128), jnp.int32),
            jax.ShapeDtypeStruct((META, 128), jnp.int32),
        ),
        in_specs=[VMEM, HBM, VMEM, VMEM, VMEM],
        out_specs=(VMEM,) * 6,
        scratch_shapes=[
            pltpu.VMEM((KVH, D, 2 * HD), bf16),
            pltpu.VMEM((KVH, D, QPK * HD), bf16),
            pltpu.VMEM((KVH, ROWS, 2 * HD), bf16),
            pltpu.VMEM((KVH, ROWS, QPK * HD), bf16),
            DMA((16,)),
            DMA((7,)),
            DMA((7,)),
            DMA((8,)),
            DMA((8,)),
            DMA((30,)),
            DMA((30,)),
            DMA,
        ],
        compiler_params=pltpu.CompilerParams(collective_id=0, has_side_effects=True, vmem_limit_bytes=24 << 20),
        name="project",
    )(hidden, w_qkv, seg_ids.reshape(-1, 128), live.reshape(-1, 128), page_table.reshape(-1, 128))

    att, pool = pl.pallas_call(
        attend,
        out_shape=(
            jax.ShapeDtypeStruct((STRIPES, ROWS, QPK * HD), bf16),
            jax.ShapeDtypeStruct((GT, 2 * HD), bf16),
        ),
        in_specs=[ANY, VMEM, VMEM, VMEM, VMEM, VMEM],
        out_specs=(VMEM, HBM),
        scratch_shapes=[
            pltpu.SMEM((META, 128), jnp.int32),
            pltpu.VMEM((2 * HD, QPK * ROWS), bf16),
            pltpu.VMEM((1, QPK * ROWS), f32),
            pltpu.VMEM((VR, QPK * ROWS), f32),
            pltpu.VMEM((BK, QPK * ROWS), f32),
            pltpu.VMEM((BK, QPK * ROWS), f32),
            DMA,
            DMA,
        ],
        compiler_params=pltpu.CompilerParams(vmem_limit_bytes=20 << 20),
        name="attend",
    )(meta, code, q, kv, kx, vt)

    mixed = pl.pallas_call(
        mix,
        out_shape=jax.ShapeDtypeStruct((ROWS, D), bf16),
        in_specs=[ANY, VMEM],
        out_specs=VMEM,
        scratch_shapes=[
            pltpu.VMEM((KVH, ROWS, QPK * HD), bf16),
            pltpu.VMEM((ROWS, D), f32),
            DMA((8,)),
            DMA((8,)),
        ],
        compiler_params=pltpu.CompilerParams(collective_id=1, has_side_effects=True, vmem_limit_bytes=12 << 20),
        name="mix",
    )(att, w_out)
    return mixed, pool.reshape(1, TOKENS // PAGE // SEQ, PAGE, 2 * HD)


def solution(mesh):
    placed = (P(("seq", "head"), None), P(), P(), P(), P(), P())
    return jax.shard_map(
        shards,
        mesh=mesh,
        in_specs=placed,
        out_specs=(P(("seq", "head"), None), P("head", "seq", None, None)),
        check_vma=False,
    )
```

```python
import functools

import jax
import jax.numpy as jnp
from jax import lax
from jax.experimental import pallas as pl
from jax.experimental.pallas import tpu as pltpu
from jax.sharding import PartitionSpec as P

D = 2048
TOKENS = 16384
KVH = 8
HD = 64
QPK = 4
PAGE = 16
SEQ = 16
SEGS = 8
ROWS = 128
GT = 1024
COLS = (QPK + 2) * HD
STRIPES = 8
BK = 512
PAD = 2 * BK
META = STRIPES + 64
EARLY = 4
NEG = -1e30
MESH = pl.DeviceIdType.MESH
bf16, f32 = jnp.bfloat16, jnp.float32


FLIP_Z = (1, 0, 0, 1, 1, 0, 0, 0)
FLIP_CORE = (0, 1, 1, 0, 1, 0, 1, 0)
FLIP_ODD = (1, 1, 1, 0, 0, 0, 0, 0)
FLIP_EVEN = (0, 0, 1, 0, 0, 1, 1, 1)


def bit(table, k):
    if isinstance(k, int):
        return table[k]
    return sum(jnp.where(k == n, 1, 0) for n in range(8) if table[n])


NT = (((1,), (1,)), ((), ()))
VR = HD + 16


def dealt(s, j):
    k, c, y, low = s // 2, s % 2, j // 2, j % 2
    odd = jnp.where((y + c + bit(FLIP_ODD, k)) % 2 == 0, 1, 3)
    even = jnp.where((y + c + bit(FLIP_EVEN, k)) % 2 == 0, 0, 2)
    x = (k + jnp.where(y < 2, odd, even)) % 4
    return (c + bit(FLIP_Z, k)) % 2 * 8 + x * 2 + (low + bit(FLIP_CORE, k)) % 2


def slot_of(s, k):
    c = (s // 8 + bit(FLIP_Z, k)) % 2
    low = (s % 2 + bit(FLIP_CORE, k)) % 2
    move = (s // 2 + 8 - k) % 4
    odd = (jnp.where(move == 3, 1, 0) + c + bit(FLIP_ODD, k)) % 2
    even = 2 + (jnp.where(move == 2, 1, 0) + c + bit(FLIP_EVEN, k)) % 2
    return c * 8 + jnp.where(move % 2 == 1, odd, even) * 2 + low


def held(s, k):
    slot = slot_of(s, k)
    return 2 * k + slot // 8, slot % 8


def project(
    hv, w, given, q_out, kv_out, kx, vt, code, meta,
    wk, wq, kvs, qs, load, a2a_s, a2a_r, q_s, q_r, g_s, g_r, loc,
):
    s, j = lax.axis_index("seq"), lax.axis_index("head")
    zh, x, c = s // 8, (s // 2) % 4, s % 2
    to = dealt(s, j)
    mine = to == s

    loads = []
    for r in range(8):
        g = lax.rem(j + r + 1, 8)
        col = pl.multiple_of(g * COLS + QPK * HD, 128)
        loads.append(pltpu.make_async_copy(w.at[:, pl.ds(col, 2 * HD)], wk.at[r], load.at[r]))
        loads[-1].start()
    for r in range(8):
        g = lax.rem(j + r + 1, 8)
        col = pl.multiple_of(g * COLS, 128)
        loads.append(pltpu.make_async_copy(w.at[:, pl.ds(col, QPK * HD)], wq.at[r], load.at[8 + r]))
        loads[-1].start()

    def block(zz, xx, cc):
        return zz * 8 + xx * 2 + cc

    right, left = lax.rem(x + 1, 4), lax.rem(x + 3, 4)
    far = lax.rem(x + 2, 4)
    peers = [(block(zh, right, c), j), (block(zh, left, c), j), (block(1 - zh, x, c), j), (block(zh, x, 1 - c), j)]

    barrier = pltpu.get_barrier_semaphore()
    for p in peers:
        pl.semaphore_signal(barrier, inc=1, device_id=p, device_id_type=MESH)
    for r in range(7):
        pl.semaphore_signal(barrier, inc=1, device_id=(s, lax.rem(j + r + 1, 8)), device_id_type=MESH)
    for k in range(STRIPES):
        own = mine & (s // 2 == k)

        @pl.when(jnp.logical_not(own))
        def _():
            pl.semaphore_signal(barrier, inc=1, device_id=held(s, k), device_id_type=MESH)

    down = lax.broadcasted_iota(jnp.int32, (128, 128), 0)
    along = lax.broadcasted_iota(jnp.int32, (128, 128), 1)
    pick = (along[:HD] == down[:HD] + HD).astype(bf16)
    marks = (down >= HD) & (down < HD + SEGS)
    mark_row = (along[:1] >= HD) & (along[:1] < HD + SEGS)

    def tables():
        code[...] = given[: TOKENS // 128]
        seg = code[...] & 15
        lane = along[:1]
        for k in range(STRIPES):
            stripe = 16 * k + slot_of(s, k)
            own = code[pl.ds(stripe, 1), :][:, :1] & 15
            before = jnp.where(seg < own, 1.0, 0.0)
            begin = jnp.sum(jnp.sum(before, axis=0, keepdims=True), axis=1, keepdims=True).astype(jnp.int32)
            blocks = lax.shift_right_logical(stripe * ROWS - begin + BK - 1, BK.bit_length() - 1)
            meta[k : k + 1, :] = jnp.where(lane == 0, blocks, own)
        at = jnp.zeros((64, 128), f32)
        for n in range(TOKENS // PAGE // 128):
            hit = given[TOKENS // 128 + n : TOKENS // 128 + n + 1, :] == 64 * s + down[:64]
            at += jnp.where(hit, (n * 128 + along[:64]).astype(f32), 0.0)
        logical = jnp.sum(at, axis=1, keepdims=True).astype(jnp.int32)
        meta[STRIPES:, :] = jnp.broadcast_to(logical, (64, 128))
        kx[:PAD] = jnp.broadcast_to(jnp.where(mark_row, NEG, 0.0), (PAD, 2 * HD)).astype(bf16)
        vt[:HD, :PAD] = jnp.zeros((HD, PAD), bf16)
        vt[HD:, :] = jnp.ones((VR - HD, PAD + TOKENS), bf16)

    def use(b, h):
        at = pl.multiple_of(b * GT + h * (GT // 2), 128)
        to = pl.multiple_of(PAD + at, 128)
        rows = kv_out[pl.ds(at, GT // 2), :]
        vt[:HD, pl.ds(to, GT // 2)] = lax.dot_general(pick, rows, NT, preferred_element_type=f32).astype(bf16)
        for n in range(GT // 2 // 128):
            row = given[pl.ds(b * (GT // 128) + h * (GT // 256) + n, 1), :]
            mark = jnp.where(marks & (row != down - HD), NEG, 0.0).T.astype(bf16)
            kx[pl.ds(to + n * 128, 128), :] = jnp.where(along[:1] < HD, rows[n * 128 : (n + 1) * 128], mark)

    def query(r):
        loads[8 + r].wait()
        qs[r] = (jnp.dot(hv[...], wq[r], preferred_element_type=f32).astype(bf16) * 0.015625).astype(bf16)

    for r in range(8):
        loads[r].wait()
        kvs[r] = jnp.dot(hv[...], wk[r], preferred_element_type=f32).astype(bf16)
    for r in range(EARLY):
        query(r)
    row0 = pl.multiple_of(s * GT + j * ROWS, ROWS)
    own_kv = pltpu.make_async_copy(kvs.at[7], kv_out.at[pl.ds(row0, ROWS)], loc)
    own_kv.start()
    pl.semaphore_wait(barrier, jnp.where(mine, 18, 19))
    sends = []
    for r in range(7):
        cp = pltpu.make_async_remote_copy(
            src_ref=kvs.at[r],
            dst_ref=kv_out.at[pl.ds(row0, ROWS)],
            send_sem=a2a_s.at[r],
            recv_sem=a2a_r.at[r],
            device_id=(s, lax.rem(j + r + 1, 8)),
            device_id_type=MESH,
        )
        cp.start()
        sends.append(cp)

    H = GT // 2
    R, L, Z, C = range(4)

    def half(b, h):
        return kv_out.at[pl.ds(pl.multiple_of(b * GT + h * H, 128), H)]

    count = [0]

    def pass_on(b, h, *to_peers):
        for peer in to_peers:
            i = count[0]
            count[0] += 1
            cp = pltpu.make_async_remote_copy(
                src_ref=half(b, h),
                dst_ref=half(b, h),
                send_sem=g_s.at[i],
                recv_sem=g_r.at[i],
                device_id=peers[peer],
                device_id_type=MESH,
            )
            cp.start()
            sends.append(cp)

    def arrived(b, h, i):
        pltpu.make_async_copy(half(b, h), half(b, h), g_r.at[i]).wait()

    slot = s // 2
    qsends = []

    def send_query(r):
        cp = pltpu.make_async_remote_copy(
            src_ref=qs.at[r],
            dst_ref=q_out.at[slot],
            send_sem=q_s.at[r],
            recv_sem=q_r.at[slot],
            device_id=(to, lax.rem(j + r + 1, 8)),
            device_id_type=MESH,
        )
        qsends.append(cp)
        if r < 7:
            cp.start()
        else:

            @pl.when(jnp.logical_not(mine))
            def _():
                cp.start()

            @pl.when(mine)
            def _():
                pltpu.make_async_copy(qs.at[7], q_out.at[slot], q_r.at[slot]).start()

    for r in range(8):
        if r >= EARLY:
            query(r)
        send_query(r)
    tables()
    own_kv.wait()
    for r in range(7):
        source = lax.rem(j + 7 - r, 8)
        there = kv_out.at[pl.ds(pl.multiple_of(s * GT + source * ROWS, ROWS), ROWS)]
        pltpu.make_async_copy(there, there, a2a_r.at[r]).wait()
    me = block(zh, x, c)
    bl, br, bf = block(zh, left, c), block(zh, right, c), block(zh, far, c)
    zm, zl, zr, zf = block(1 - zh, x, c), block(1 - zh, left, c), block(1 - zh, right, c), block(1 - zh, far, c)
    pass_on(me, 0, R, Z)
    pass_on(me, 1, L, Z)
    pass_on(me, 1, R)
    pass_on(me, 0, L, C)
    pass_on(me, 1, C)
    d = 1 - c
    ome, ol, or_, of = block(zh, x, d), block(zh, left, d), block(zh, right, d), block(zh, far, d)
    oz, ozl, ozr, ozf = block(1 - zh, x, d), block(1 - zh, left, d), block(1 - zh, right, d), block(1 - zh, far, d)
    arrived(bl, 0, 0)
    pass_on(bl, 0, R, C)
    arrived(br, 1, 2)
    pass_on(br, 1, L, C)
    arrived(zm, 0, 1)
    pass_on(zm, 0, R, L, C)
    use(me, 0)
    use(me, 1)
    arrived(zm, 1, 3)
    pass_on(zm, 1, R, L, C)
    arrived(bl, 1, 4)
    pass_on(bl, 1, C)
    arrived(br, 0, 5)
    pass_on(br, 0, C)
    use(bl, 0)
    use(br, 1)
    arrived(bf, 0, 8)
    pass_on(bf, 0, Z, C)
    arrived(bf, 1, 10)
    pass_on(bf, 1, Z, C)

    def other(b, h, i):
        arrived(b, h, i)
        use(b, h)

    use(zm, 0)
    use(zm, 1)
    use(bl, 1)
    use(br, 0)
    other(ome, 0, 6)
    other(ome, 1, 7)
    other(ol, 0, 9)
    other(or_, 1, 11)
    other(oz, 0, 14)
    arrived(zl, 0, 12)
    pass_on(zl, 0, C)
    arrived(zr, 0, 13)
    pass_on(zr, 0, C)
    other(oz, 1, 17)
    other(ol, 1, 18)
    other(or_, 0, 19)
    use(bf, 0)
    use(bf, 1)
    other(of, 0, 21)
    other(of, 1, 23)
    arrived(zf, 0, 20)
    pass_on(zf, 0, C)
    use(zl, 0)
    use(zr, 0)
    arrived(zl, 1, 15)
    pass_on(zl, 1, C)
    arrived(zr, 1, 16)
    pass_on(zr, 1, C)
    arrived(zf, 1, 22)
    pass_on(zf, 1, C)
    use(zf, 0)
    other(ozl, 0, 24)
    other(ozr, 0, 25)
    use(zl, 1)
    use(zr, 1)
    other(ozf, 0, 26)
    use(zf, 1)
    other(ozl, 1, 27)
    other(ozr, 1, 28)
    other(ozf, 1, 29)

    for k in range(STRIPES):
        pltpu.make_async_copy(q_out.at[k], q_out.at[k], q_r.at[k]).wait()
    for cp in sends + qsends[:7]:
        cp.wait_send()

    @pl.when(jnp.logical_not(mine))
    def _():
        qsends[7].wait_send()


def attend(meta_in, code, q, kv, kx, vt, att, pool, meta, qt, m, acc, sa, sb, sem, page_sem):
    s = lax.axis_index("seq")
    fetch = pltpu.make_async_copy(meta_in, meta, sem)
    fetch.start()
    down = lax.broadcasted_iota(jnp.int32, (128, 128), 0)
    along = lax.broadcasted_iota(jnp.int32, (128, 128), 1)

    def peak(sc):
        return jnp.max(sc.reshape(sc.shape[0] // 8, 8, sc.shape[1]), axis=0)

    def scores(first):
        keys = kx[pl.ds(pl.multiple_of(first, 128), BK), :]
        return jnp.dot(keys, qt[...], preferred_element_type=f32)

    fetch.wait()

    @pl.loop(0, TOKENS // PAGE // SEQ)
    def _(i):
        at = pl.multiple_of(meta[STRIPES + i, 0] * PAGE, PAGE)
        to = pl.multiple_of(i * PAGE, PAGE)
        pltpu.make_async_copy(kv.at[pl.ds(at, PAGE)], pool.at[pl.ds(to, PAGE)], page_sem).start()

    @pl.loop(0, STRIPES)
    def _(k):
        stripe = 16 * k + slot_of(s, k)
        own = meta[k, 1]
        here = pl.multiple_of(PAD + stripe * ROWS, 128)
        for c in range(0, QPK, 2):
            t = q[k, :, c * HD : (c + 2) * HD].T
            qt[:HD, c * ROWS : (c + 1) * ROWS] = t[:HD]
            qt[:HD, (c + 1) * ROWS : (c + 2) * ROWS] = t[HD:]
        qt[HD:, :] = (lax.broadcasted_iota(jnp.int32, (HD, QPK * ROWS), 0) == own).astype(bf16)

        sc = scores(here - BK)
        sa[...] = sc
        near = peak(sc)

        row = code[pl.ds(stripe, 1), :]
        ct = jnp.broadcast_to(row, (ROWS, ROWS))
        cu = ct.T
        allowed = ((cu & 15) == (ct & 15)) & (down <= along) & ((cu < 16) | (down == along))
        same = (row & 15) == own
        sc = jnp.dot(kx[pl.ds(here, ROWS), :HD], qt[:HD, :], preferred_element_type=f32)
        sc = jnp.concatenate(
            [jnp.where(allowed, sc[:, c * ROWS : (c + 1) * ROWS], NEG) for c in range(QPK)], axis=1
        )
        top = jnp.max(peak(sc), axis=0, keepdims=True)
        p = jnp.exp(sc - top).astype(bf16)
        acc[...] = jnp.dot(vt[:, pl.ds(here, ROWS)], p, preferred_element_type=f32)
        m[...] = jnp.where(jnp.concatenate([same] * QPK, axis=1), top, -NEG)

        def weigh(b, src, peaks, dst=None):
            first = here - (b + 1) * BK
            old = m[...]
            top = jnp.maximum(old, jnp.max(peaks, axis=0, keepdims=True))
            m[...] = top
            if dst is not None:
                sc = scores(first - BK)
                dst[...] = sc
            p = jnp.exp(src[...] - top).astype(bf16)
            part = jnp.dot(vt[:, pl.ds(pl.multiple_of(first, 128), BK)], p, preferred_element_type=f32)
            acc[...] = acc[...] * jnp.exp(old - top) + part
            return None if dst is None else peak(sc)

        def pair(i, peaks):
            peaks = weigh(2 * i, sa, peaks, sb)
            return weigh(2 * i + 1, sb, peaks, sa)

        blocks = meta[k, 0]
        last = lax.fori_loop(0, blocks // 2, pair, near)

        @pl.when(blocks % 2 == 1)
        def _():
            weigh(blocks - 1, sa, last)

        for c in range(0, QPK, 2):
            one, two = slice(c * ROWS, (c + 1) * ROWS), slice((c + 1) * ROWS, (c + 2) * ROWS)
            done = jnp.concatenate(
                [acc[:HD, one] / acc[HD : HD + 1, one], acc[:HD, two] / acc[HD : HD + 1, two]], axis=0
            )
            att[k, :, c * HD : (c + 2) * HD] = done.T.astype(bf16)

    pltpu.make_async_copy(kv.at[pl.ds(0, GT)], pool, page_sem).wait()


def mix(att, w, out, got, acc, a_s, a_r):
    s, j = lax.axis_index("seq"), lax.axis_index("head")
    to = dealt(s, j)
    mine = to == s
    barrier = pltpu.get_barrier_semaphore()
    for r in range(8):
        h = lax.rem(j + r + 1, 8)
        if r < 7:
            pl.semaphore_signal(barrier, inc=1, device_id=(to, h), device_id_type=MESH)
        else:

            @pl.when(jnp.logical_not(mine))
            def _():
                pl.semaphore_signal(barrier, inc=1, device_id=(to, h), device_id_type=MESH)

    pl.semaphore_wait(barrier, jnp.where(mine, 7, 8))

    copies = []
    for k in range(STRIPES):
        own = mine & (s // 2 == k)
        cp = pltpu.make_async_remote_copy(
            src_ref=att.at[k],
            dst_ref=got.at[j],
            send_sem=a_s.at[k],
            recv_sem=a_r.at[j],
            device_id=held(s, k),
            device_id_type=MESH,
        )
        copies.append((own, cp))

        @pl.when(jnp.logical_not(own))
        def _():
            cp.start()

        @pl.when(own)
        def _():
            pltpu.make_async_copy(att.at[k], got.at[j], a_r.at[j]).start()

    for r in range(8):
        h = lax.rem(j + 8 - r, 8)
        pltpu.make_async_copy(got.at[h], got.at[h], a_r.at[h]).wait()
        part = jnp.dot(
            got[h], w[pl.ds(pl.multiple_of(h * QPK * HD, QPK * HD), QPK * HD), :], preferred_element_type=f32
        )
        if r == 0:
            acc[...] = part
        elif r < 7:
            acc[...] += part
        else:
            out[...] = (acc[...] + part).astype(bf16)
    for own, cp in copies:

        @pl.when(jnp.logical_not(own))
        def _():
            cp.wait_send()


ANY = pl.BlockSpec(memory_space=pl.ANY)
SMEM = pl.BlockSpec(memory_space=pltpu.SMEM)
VMEM = pl.BlockSpec(memory_space=pltpu.VMEM)
DMA = pltpu.SemaphoreType.DMA


HBM = pl.BlockSpec(memory_space=pltpu.HBM)


def projected(hidden, w_qkv, given):
    return pl.pallas_call(
        project,
        out_shape=(
            jax.ShapeDtypeStruct((STRIPES, ROWS, QPK * HD), bf16),
            jax.ShapeDtypeStruct((TOKENS, 2 * HD), bf16),
            jax.ShapeDtypeStruct((PAD + TOKENS, 2 * HD), bf16),
            jax.ShapeDtypeStruct((VR, PAD + TOKENS), bf16),
            jax.ShapeDtypeStruct((TOKENS // 128, 128), jnp.int32),
            jax.ShapeDtypeStruct((META, 128), jnp.int32),
        ),
        in_specs=[VMEM, HBM, VMEM],
        out_specs=(VMEM,) * 6,
        scratch_shapes=[
            pltpu.VMEM((KVH, D, 2 * HD), bf16),
            pltpu.VMEM((KVH, D, QPK * HD), bf16),
            pltpu.VMEM((KVH, ROWS, 2 * HD), bf16),
            pltpu.VMEM((KVH, ROWS, QPK * HD), bf16),
            DMA((16,)),
            DMA((7,)),
            DMA((7,)),
            DMA((8,)),
            DMA((8,)),
            DMA((30,)),
            DMA((30,)),
            DMA,
        ],
        compiler_params=pltpu.CompilerParams(collective_id=0, has_side_effects=True, vmem_limit_bytes=34 << 20),
        name="project",
    )(hidden, w_qkv, given)


def shards(hidden, w_qkv, w_out, seg_ids, live, page_table):
    given = jnp.concatenate([seg_ids + 16 * (1 - live), page_table]).reshape(-1, 128)
    q, kv, kx, vt, code, meta = projected(hidden, w_qkv, given)
    att, pool = pl.pallas_call(
        attend,
        out_shape=(
            jax.ShapeDtypeStruct((STRIPES, ROWS, QPK * HD), bf16),
            jax.ShapeDtypeStruct((GT, 2 * HD), bf16),
        ),
        in_specs=[ANY, VMEM, VMEM, VMEM, VMEM, VMEM],
        out_specs=(VMEM, HBM),
        scratch_shapes=[
            pltpu.SMEM((META, 128), jnp.int32),
            pltpu.VMEM((2 * HD, QPK * ROWS), bf16),
            pltpu.VMEM((1, QPK * ROWS), f32),
            pltpu.VMEM((VR, QPK * ROWS), f32),
            pltpu.VMEM((BK, QPK * ROWS), f32),
            pltpu.VMEM((BK, QPK * ROWS), f32),
            DMA,
            DMA,
        ],
        compiler_params=pltpu.CompilerParams(vmem_limit_bytes=20 << 20),
        name="attend",
    )(meta, code, q, kv, kx, vt)

    mixed = pl.pallas_call(
        mix,
        out_shape=jax.ShapeDtypeStruct((ROWS, D), bf16),
        in_specs=[ANY, VMEM],
        out_specs=VMEM,
        scratch_shapes=[
            pltpu.VMEM((KVH, ROWS, QPK * HD), bf16),
            pltpu.VMEM((ROWS, D), f32),
            DMA((8,)),
            DMA((8,)),
        ],
        compiler_params=pltpu.CompilerParams(collective_id=1, has_side_effects=True, vmem_limit_bytes=12 << 20),
        name="mix",
    )(att, w_out)
    return mixed, pool.reshape(1, TOKENS // PAGE // SEQ, PAGE, 2 * HD)


def solution(mesh):
    placed = (P(("seq", "head"), None), P(), P(), P(), P(), P())
    return jax.shard_map(
        shards,
        mesh=mesh,
        in_specs=placed,
        out_specs=(P(("seq", "head"), None), P("head", "seq", None, None)),
        check_vma=False,
    )
```

```python
import functools

import jax
import jax.numpy as jnp
from jax import lax
from jax.experimental import pallas as pl
from jax.experimental.pallas import tpu as pltpu
from jax.sharding import PartitionSpec as P

D = 2048
TOKENS = 16384
KVH = 8
HD = 64
QPK = 4
PAGE = 16
SEQ = 16
SEGS = 8
ROWS = 128
GT = 1024
COLS = (QPK + 2) * HD
STRIPES = 8
BK = 512
PAD = 2 * BK
ITEMS = STRIPES * (TOKENS // BK) + 8
META = STRIPES + 64
CHUNKS = 2
CH = GT // CHUNKS
EARLY = 4
NEG = -1e30
MESH = pl.DeviceIdType.MESH
bf16, f32 = jnp.bfloat16, jnp.float32


FLIP_Z = (1, 0, 0, 1, 1, 0, 0, 0)
FLIP_CORE = (0, 1, 1, 0, 1, 0, 1, 0)
FLIP_ODD = (1, 1, 1, 0, 0, 0, 0, 0)
FLIP_EVEN = (0, 0, 1, 0, 0, 1, 1, 1)


def bit(table, k):
    if isinstance(k, int):
        return table[k]
    return sum(jnp.where(k == n, 1, 0) for n in range(8) if table[n])


NT = (((1,), (1,)), ((), ()))
VR = HD + 16


def dealt(s, j):
    k, c, y, low = s // 2, s % 2, j // 2, j % 2
    odd = jnp.where((y + c + bit(FLIP_ODD, k)) % 2 == 0, 1, 3)
    even = jnp.where((y + c + bit(FLIP_EVEN, k)) % 2 == 0, 0, 2)
    x = (k + jnp.where(y < 2, odd, even)) % 4
    return (c + bit(FLIP_Z, k)) % 2 * 8 + x * 2 + (low + bit(FLIP_CORE, k)) % 2


def slot_of(s, k):
    c = (s // 8 + bit(FLIP_Z, k)) % 2
    low = (s % 2 + bit(FLIP_CORE, k)) % 2
    move = (s // 2 + 8 - k) % 4
    odd = (jnp.where(move == 3, 1, 0) + c + bit(FLIP_ODD, k)) % 2
    even = 2 + (jnp.where(move == 2, 1, 0) + c + bit(FLIP_EVEN, k)) % 2
    return c * 8 + jnp.where(move % 2 == 1, odd, even) * 2 + low


def held(s, k):
    slot = slot_of(s, k)
    return 2 * k + slot // 8, slot % 8


def project(
    hv, w, given, q_out, kv_out, kx, vt, code, meta,
    wk, wq, kvs, qs, load, a2a_s, a2a_r, q_s, q_r, g_s, g_r, loc,
):
    s, j = lax.axis_index("seq"), lax.axis_index("head")
    zh, x, c = s // 8, (s // 2) % 4, s % 2
    to = dealt(s, j)
    mine = to == s

    loads = []
    for r in range(8):
        g = lax.rem(j + r + 1, 8)
        col = pl.multiple_of(g * COLS + QPK * HD, 128)
        loads.append(pltpu.make_async_copy(w.at[:, pl.ds(col, 2 * HD)], wk.at[r], load.at[r]))
        loads[-1].start()
    for r in range(8):
        g = lax.rem(j + r + 1, 8)
        col = pl.multiple_of(g * COLS, 128)
        loads.append(pltpu.make_async_copy(w.at[:, pl.ds(col, QPK * HD)], wq.at[r], load.at[8 + r]))
        loads[-1].start()

    def block(zz, xx, cc):
        return zz * 8 + xx * 2 + cc

    right, left = lax.rem(x + 1, 4), lax.rem(x + 3, 4)
    far = lax.rem(x + 2, 4)
    peers = [(block(zh, right, c), j), (block(zh, left, c), j), (block(1 - zh, x, c), j), (block(zh, x, 1 - c), j)]

    barrier = pltpu.get_barrier_semaphore()
    for p in peers:
        pl.semaphore_signal(barrier, inc=1, device_id=p, device_id_type=MESH)
    for r in range(7):
        pl.semaphore_signal(barrier, inc=1, device_id=(s, lax.rem(j + r + 1, 8)), device_id_type=MESH)
    for k in range(STRIPES):
        own = mine & (s // 2 == k)

        @pl.when(jnp.logical_not(own))
        def _():
            pl.semaphore_signal(barrier, inc=1, device_id=held(s, k), device_id_type=MESH)

    down = lax.broadcasted_iota(jnp.int32, (128, 128), 0)
    along = lax.broadcasted_iota(jnp.int32, (128, 128), 1)
    pick = (along[:HD] == down[:HD] + HD).astype(bf16)
    marks = (down >= HD) & (down < HD + SEGS)
    mark_row = (along[:1] >= HD) & (along[:1] < HD + SEGS)

    def tables():
        code[...] = given[...] & 31
        seg = code[...] & 15
        lane = along[:1]
        for k in range(STRIPES):
            stripe = 16 * k + slot_of(s, k)
            own = code[pl.ds(stripe, 1), :][:, :1] & 15
            before = jnp.where(seg < own, 1.0, 0.0)
            begin = jnp.sum(jnp.sum(before, axis=0, keepdims=True), axis=1, keepdims=True).astype(jnp.int32)
            blocks = lax.shift_right_logical(stripe * ROWS - begin + BK - 1, BK.bit_length() - 1)
            meta[k : k + 1, :] = jnp.where(lane == 0, blocks, own)
        at = jnp.zeros((64, 128), f32)
        for n in range(TOKENS // PAGE // 128):
            hit = lax.shift_right_logical(given[n : n + 1, :], 5) == 64 * s + down[:64]
            at += jnp.where(hit, (n * 128 + along[:64]).astype(f32), 0.0)
        logical = jnp.sum(at, axis=1, keepdims=True).astype(jnp.int32)
        meta[STRIPES:, :] = jnp.broadcast_to(logical, (64, 128))
        kx[:PAD] = jnp.broadcast_to(jnp.where(mark_row, NEG, 0.0), (PAD, 2 * HD)).astype(bf16)
        vt[:HD, :PAD] = jnp.zeros((HD, PAD), bf16)
        vt[HD:, :] = jnp.ones((VR - HD, PAD + TOKENS), bf16)

    def use(b, h):
        at = pl.multiple_of(b * GT + h * CH, 128)
        to = pl.multiple_of(PAD + at, 128)
        rows = kv_out[pl.ds(at, CH), :]
        vt[:HD, pl.ds(to, CH)] = lax.dot_general(pick, rows, NT, preferred_element_type=f32).astype(bf16)
        for n in range(CH // 128):
            row = code[pl.ds(b * (GT // 128) + h * (CH // 128) + n, 1), :]
            mark = jnp.where(marks & (row != down - HD), NEG, 0.0).T.astype(bf16)
            kx[pl.ds(to + n * 128, 128), :] = jnp.where(along[:1] < HD, rows[n * 128 : (n + 1) * 128], mark)

    def query(r):
        loads[8 + r].wait()
        qs[r] = (jnp.dot(hv[...], wq[r], preferred_element_type=f32).astype(bf16) * 0.015625).astype(bf16)

    for r in range(8):
        loads[r].wait()
        kvs[r] = jnp.dot(hv[...], wk[r], preferred_element_type=f32).astype(bf16)
    for r in range(EARLY):
        query(r)
    row0 = pl.multiple_of(s * GT + j * ROWS, ROWS)
    own_kv = pltpu.make_async_copy(kvs.at[7], kv_out.at[pl.ds(row0, ROWS)], loc)
    own_kv.start()
    pl.semaphore_wait(barrier, jnp.where(mine, 18, 19))
    sends = []
    for r in range(7):
        cp = pltpu.make_async_remote_copy(
            src_ref=kvs.at[r],
            dst_ref=kv_out.at[pl.ds(row0, ROWS)],
            send_sem=a2a_s.at[r],
            recv_sem=a2a_r.at[r],
            device_id=(s, lax.rem(j + r + 1, 8)),
            device_id_type=MESH,
        )
        cp.start()
        sends.append(cp)

    R, L, Z, C = range(4)
    held_at = {}

    def half(b, h):
        return kv_out.at[pl.ds(pl.multiple_of(held_at[b] * GT + h * CH, 128), CH)]

    copies = {}

    def pass_on(b, h, *to_peers):
        for peer in to_peers:
            i = len(copies)
            copies[b, h, peer] = i
            cp = pltpu.make_async_remote_copy(
                src_ref=half(b, h),
                dst_ref=half(b, h),
                send_sem=g_s.at[i],
                recv_sem=g_r.at[i],
                device_id=peers[peer],
                device_id_type=MESH,
            )
            cp.start()
            sends.append(cp)

    def arrived(b, h, sent, peer):
        pltpu.make_async_copy(half(b, h), half(b, h), g_r.at[copies[sent, h, peer]]).wait()

    slot = s // 2
    qsends = []

    def send_query(r):
        cp = pltpu.make_async_remote_copy(
            src_ref=qs.at[r],
            dst_ref=q_out.at[slot],
            send_sem=q_s.at[r],
            recv_sem=q_r.at[slot],
            device_id=(to, lax.rem(j + r + 1, 8)),
            device_id_type=MESH,
        )
        qsends.append(cp)
        if r < 7:
            cp.start()
        else:

            @pl.when(jnp.logical_not(mine))
            def _():
                cp.start()

            @pl.when(mine)
            def _():
                pltpu.make_async_copy(qs.at[7], q_out.at[slot], q_r.at[slot]).start()

    for r in range(8):
        if r >= EARLY:
            query(r)
        send_query(r)
    tables()
    own_kv.wait()
    for r in range(7):
        source = lax.rem(j + 7 - r, 8)
        there = kv_out.at[pl.ds(pl.multiple_of(s * GT + source * ROWS, ROWS), ROWS)]
        pltpu.make_async_copy(there, there, a2a_r.at[r]).wait()
    places = (("m", x), ("l", left), ("r", right), ("f", far))
    for half_z, zz in (("o", zh), ("z", 1 - zh)):
        for core, cc in (("", c), ("c", 1 - c)):
            for name, xx in places:
                held_at[half_z + name + core] = block(zz, xx, cc)
    low, high = range(CHUNKS // 2), range(CHUNKS // 2, CHUNKS)
    for h in low:
        pass_on("om", h, R, Z)
    for h in high:
        pass_on("om", h, L, Z)
    for h in high:
        pass_on("om", h, R)
    for h in low:
        pass_on("om", h, L, C)
    for h in high:
        pass_on("om", h, C)

    def ready(b, *chunks):
        for h in chunks:
            use(held_at[b], h)

    def other(b, *chunks):
        for h in chunks:
            arrived(b + "c", h, b, C)
            use(held_at[b + "c"], h)

    for h, g in zip(low, high, strict=True):
        arrived("ol", h, "om", R)
        pass_on("ol", h, R, C)
        arrived("or", g, "om", L)
        pass_on("or", g, L, C)
        ready("om", h)
    for h in (*low, *high):
        arrived("zm", h, "om", Z)
        pass_on("zm", h, R, L, C)
        if h in high:
            ready("om", h)
    for h, g in zip(low, high, strict=True):
        arrived("ol", g, "om", R)
        pass_on("ol", g, C)
        arrived("or", h, "om", L)
        pass_on("or", h, C)
        ready("ol", h)
        ready("or", g)
    for h, g in zip(low, high, strict=True):
        arrived("of", h, "ol", R)
        pass_on("of", h, Z, C)
        arrived("of", g, "or", L)
        pass_on("of", g, Z, C)
        ready("zm", h, g)
        other("om", h, g)
    ready("ol", *high)
    ready("or", *low)
    other("ol", *low)
    other("or", *high)
    other("zm", *low)
    for h in (*low, *high):
        arrived("zl", h, "zm", R)
        pass_on("zl", h, C)
        arrived("zr", h, "zm", L)
        pass_on("zr", h, C)
        if h in low:
            other("zm", h + CHUNKS // 2)
            other("ol", h + CHUNKS // 2)
            other("or", h)
        else:
            ready("of", h - CHUNKS // 2, h)
            other("of", h - CHUNKS // 2, h)
            ready("zl", h - CHUNKS // 2)
            ready("zr", h - CHUNKS // 2)
    for h, g in zip(low, high, strict=True):
        arrived("zf", h, "of", Z)
        pass_on("zf", h, C)
        ready("zl", g)
        arrived("zf", g, "of", Z)
        pass_on("zf", g, C)
        ready("zr", g)
        other("zl", h)
        other("zr", h)
    ready("zf", *low, *high)
    other("zl", *high)
    other("zr", *high)
    other("zf", *low, *high)

    for k in range(STRIPES):
        pltpu.make_async_copy(q_out.at[k], q_out.at[k], q_r.at[k]).wait()
    for cp in sends + qsends[:7]:
        cp.wait_send()

    @pl.when(jnp.logical_not(mine))
    def _():
        qsends[7].wait_send()


BATCH = 8


def attend(meta_in, code, q, kv, kx, vt, att, pool, meta, item_k, item_at, qt, m, acc, sa, sb, sem, page_sem):
    s = lax.axis_index("seq")
    fetch = pltpu.make_async_copy(meta_in, meta, sem)
    fetch.start()
    down = lax.broadcasted_iota(jnp.int32, (128, 128), 0)
    along = lax.broadcasted_iota(jnp.int32, (128, 128), 1)
    wide = QPK * ROWS
    fetch.wait()

    def place(k):
        return pl.multiple_of(PAD + (16 * k + slot_of(s, k)) * ROWS, 128)

    def stripe_items(k, n):
        here = place(k)

        def one(b, n):
            item_k[n] = k
            item_at[n] = here - (b + 1) * BK
            return n + 1

        return lax.fori_loop(0, meta[k, 0], one, n)

    total = lax.fori_loop(0, STRIPES, stripe_items, 0)
    for n in range(3):
        item_k[total + n] = STRIPES - 1
        item_at[total + n] = 0

    def peak(sc):
        return jnp.max(sc.reshape(sc.shape[0] // 8, 8, sc.shape[1]), axis=0)

    @pl.loop(0, STRIPES // BATCH)
    def _(group):
        for n in range(64 * BATCH // STRIPES):
            i = group * (64 * BATCH // STRIPES) + n
            at = pl.multiple_of(meta[STRIPES + i, 0] * PAGE, PAGE)
            to = pl.multiple_of(i * PAGE, PAGE)
            pltpu.make_async_copy(kv.at[pl.ds(at, PAGE)], pool.at[pl.ds(to, PAGE)], page_sem).start()
        parts, same = [], []
        for n in range(BATCH):
            k = group * BATCH + n
            own = meta[k, 1]
            here = place(k)
            tq = [q[k, :, c * HD : (c + 2) * HD].T for c in range(0, QPK, 2)]
            tq = jnp.concatenate([h for t in tq for h in (t[:HD], t[HD:])], axis=1)
            qt[k, :HD, :] = tq
            qt[k, HD:, :] = (lax.broadcasted_iota(jnp.int32, (HD, wide), 0) == own).astype(bf16)
            row = code[pl.ds((here - PAD) // 128, 1), :]
            ct = jnp.broadcast_to(row, (ROWS, ROWS))
            cu = ct.T
            allowed = ((cu & 15) == (ct & 15)) & (down <= along) & ((cu < 16) | (down == along))
            sc = jnp.dot(kx[pl.ds(here, ROWS), :HD], tq, preferred_element_type=f32)
            parts += [jnp.where(allowed, sc[:, c * ROWS : (c + 1) * ROWS], NEG) for c in range(QPK)]
            same += [(row & 15) == own] * QPK
        sc = jnp.concatenate(parts, axis=1)
        top = jnp.max(peak(sc), axis=0, keepdims=True)
        p = jnp.exp(sc - top).astype(bf16)
        start = jnp.where(jnp.concatenate(same, axis=1), top, -NEG)
        for n in range(BATCH):
            k = group * BATCH + n
            cols = slice(n * wide, (n + 1) * wide)
            acc[k] = jnp.dot(vt[:, pl.ds(place(k), ROWS)], p[:, cols], preferred_element_type=f32)
            m[k] = start[:, cols]

    def scores(n):
        keys = kx[pl.ds(pl.multiple_of(item_at[n], 128), BK), :]
        return jnp.dot(keys, qt[item_k[n]], preferred_element_type=f32)

    def weigh(n, src, dst, peaks):
        k = item_k[n]
        old = m[k]
        top = jnp.maximum(old, jnp.max(peaks, axis=0, keepdims=True))
        m[k] = top
        sc = scores(n + 1)
        dst[...] = sc
        p = jnp.exp(src[...] - top).astype(bf16)
        part = jnp.dot(vt[:, pl.ds(pl.multiple_of(item_at[n], 128), BK)], p, preferred_element_type=f32)
        acc[k] = acc[k] * jnp.exp(old - top) + part
        return peak(sc)

    def pair(i, peaks):
        peaks = weigh(2 * i, sa, sb, peaks)
        return weigh(2 * i + 1, sb, sa, peaks)

    sc = scores(0)
    sa[...] = sc
    lax.fori_loop(0, (total + 1) // 2, pair, peak(sc))

    @pl.loop(0, STRIPES // BATCH)
    def _(group):
        for n in range(BATCH):
            k = group * BATCH + n
            done = acc[k, :HD, :] / acc[k, HD : HD + 1, :]
            for c in range(0, QPK, 2):
                two = [done[:, (c + d) * ROWS : (c + d + 1) * ROWS] for d in range(2)]
                att[k, :, c * HD : (c + 2) * HD] = jnp.concatenate(two, axis=0).T.astype(bf16)

    pltpu.make_async_copy(kv.at[pl.ds(0, GT)], pool, page_sem).wait()


def mix(att, w, out, got, acc, a_s, a_r):
    s, j = lax.axis_index("seq"), lax.axis_index("head")
    to = dealt(s, j)
    mine = to == s
    barrier = pltpu.get_barrier_semaphore()
    for r in range(8):
        h = lax.rem(j + r + 1, 8)
        if r < 7:
            pl.semaphore_signal(barrier, inc=1, device_id=(to, h), device_id_type=MESH)
        else:

            @pl.when(jnp.logical_not(mine))
            def _():
                pl.semaphore_signal(barrier, inc=1, device_id=(to, h), device_id_type=MESH)

    pl.semaphore_wait(barrier, jnp.where(mine, 7, 8))

    copies = []
    for k in range(STRIPES):
        own = mine & (s // 2 == k)
        cp = pltpu.make_async_remote_copy(
            src_ref=att.at[k],
            dst_ref=got.at[j],
            send_sem=a_s.at[k],
            recv_sem=a_r.at[j],
            device_id=held(s, k),
            device_id_type=MESH,
        )
        copies.append((own, cp))

        @pl.when(jnp.logical_not(own))
        def _():
            cp.start()

        @pl.when(own)
        def _():
            pltpu.make_async_copy(att.at[k], got.at[j], a_r.at[j]).start()

    for r in range(8):
        h = lax.rem(j + 8 - r, 8)
        pltpu.make_async_copy(got.at[h], got.at[h], a_r.at[h]).wait()
        part = jnp.dot(
            got[h], w[pl.ds(pl.multiple_of(h * QPK * HD, QPK * HD), QPK * HD), :], preferred_element_type=f32
        )
        if r == 0:
            acc[...] = part
        elif r < 7:
            acc[...] += part
        else:
            out[...] = (acc[...] + part).astype(bf16)
    for own, cp in copies:

        @pl.when(jnp.logical_not(own))
        def _():
            cp.wait_send()


ANY = pl.BlockSpec(memory_space=pl.ANY)
SMEM = pl.BlockSpec(memory_space=pltpu.SMEM)
VMEM = pl.BlockSpec(memory_space=pltpu.VMEM)
DMA = pltpu.SemaphoreType.DMA


HBM = pl.BlockSpec(memory_space=pltpu.HBM)


def projected(hidden, w_qkv, given):
    return pl.pallas_call(
        project,
        out_shape=(
            jax.ShapeDtypeStruct((STRIPES, ROWS, QPK * HD), bf16),
            jax.ShapeDtypeStruct((TOKENS, 2 * HD), bf16),
            jax.ShapeDtypeStruct((PAD + TOKENS, 2 * HD), bf16),
            jax.ShapeDtypeStruct((VR, PAD + TOKENS), bf16),
            jax.ShapeDtypeStruct((TOKENS // 128, 128), jnp.int32),
            jax.ShapeDtypeStruct((META, 128), jnp.int32),
        ),
        in_specs=[VMEM, HBM, VMEM],
        out_specs=(VMEM,) * 6,
        scratch_shapes=[
            pltpu.VMEM((KVH, D, 2 * HD), bf16),
            pltpu.VMEM((KVH, D, QPK * HD), bf16),
            pltpu.VMEM((KVH, ROWS, 2 * HD), bf16),
            pltpu.VMEM((KVH, ROWS, QPK * HD), bf16),
            DMA((16,)),
            DMA((7,)),
            DMA((7,)),
            DMA((8,)),
            DMA((8,)),
            DMA((15 * CHUNKS,)),
            DMA((15 * CHUNKS,)),
            DMA,
        ],
        compiler_params=pltpu.CompilerParams(collective_id=0, has_side_effects=True, vmem_limit_bytes=34 << 20),
        name="project",
    )(hidden, w_qkv, given)


def shards(hidden, w_qkv, w_out, seg_ids, live, page_table):
    pages = jnp.pad(page_table, (0, TOKENS - TOKENS // PAGE))
    given = (seg_ids + 16 * (1 - live) + 32 * pages).reshape(-1, 128)
    q, kv, kx, vt, code, meta = projected(hidden, w_qkv, given)
    att, pool = pl.pallas_call(
        attend,
        out_shape=(
            jax.ShapeDtypeStruct((STRIPES, ROWS, QPK * HD), bf16),
            jax.ShapeDtypeStruct((GT, 2 * HD), bf16),
        ),
        in_specs=[ANY, VMEM, VMEM, VMEM, VMEM, VMEM],
        out_specs=(VMEM, HBM),
        scratch_shapes=[
            pltpu.SMEM((META, 128), jnp.int32),
            pltpu.SMEM((ITEMS,), jnp.int32),
            pltpu.SMEM((ITEMS,), jnp.int32),
            pltpu.VMEM((STRIPES, 2 * HD, QPK * ROWS), bf16),
            pltpu.VMEM((STRIPES, 1, QPK * ROWS), f32),
            pltpu.VMEM((STRIPES, VR, QPK * ROWS), f32),
            pltpu.VMEM((BK, QPK * ROWS), f32),
            pltpu.VMEM((BK, QPK * ROWS), f32),
            DMA,
            DMA,
        ],
        compiler_params=pltpu.CompilerParams(vmem_limit_bytes=20 << 20),
        name="attend",
    )(meta, code, q, kv, kx, vt)

    mixed = pl.pallas_call(
        mix,
        out_shape=jax.ShapeDtypeStruct((ROWS, D), bf16),
        in_specs=[ANY, VMEM],
        out_specs=VMEM,
        scratch_shapes=[
            pltpu.VMEM((KVH, ROWS, QPK * HD), bf16),
            pltpu.VMEM((ROWS, D), f32),
            DMA((8,)),
            DMA((8,)),
        ],
        compiler_params=pltpu.CompilerParams(collective_id=1, has_side_effects=True, vmem_limit_bytes=12 << 20),
        name="mix",
    )(att, w_out)
    return mixed, pool.reshape(1, TOKENS // PAGE // SEQ, PAGE, 2 * HD)


def solution(mesh):
    placed = (P(("seq", "head"), None), P(), P(), P(), P(), P())
    return jax.shard_map(
        shards,
        mesh=mesh,
        in_specs=placed,
        out_specs=(P(("seq", "head"), None), P("head", "seq", None, None)),
        check_vma=False,
    )
```

```python
import functools

import jax
import jax.numpy as jnp
from jax import lax
from jax.experimental import pallas as pl
from jax.experimental.pallas import tpu as pltpu
from jax.sharding import PartitionSpec as P

D = 2048
TOKENS = 16384
KVH = 8
HD = 64
QPK = 4
PAGE = 16
SEQ = 16
SEGS = 8
ROWS = 128
GT = 1024
COLS = (QPK + 2) * HD
STRIPES = 8
BK = 512
PAD = 2 * BK
ITEMS = STRIPES * (TOKENS // BK) + 8
META = STRIPES + 64
CHUNKS = 2
CH = GT // CHUNKS
FIRST = 3
NEG = -1e30
MESH = pl.DeviceIdType.MESH
bf16, f32 = jnp.bfloat16, jnp.float32


FLIP_Z = (1, 0, 0, 1, 1, 0, 0, 0)
FLIP_CORE = (0, 1, 1, 0, 1, 0, 1, 0)
FLIP_ODD = (1, 1, 1, 0, 0, 0, 0, 0)
FLIP_EVEN = (0, 0, 1, 0, 0, 1, 1, 1)


def bit(table, k):
    if isinstance(k, int):
        return table[k]
    return sum(jnp.where(k == n, 1, 0) for n in range(8) if table[n])


NT = (((1,), (1,)), ((), ()))
VR = HD + 16


def dealt(s, j):
    k, c, y, low = s // 2, s % 2, j // 2, j % 2
    odd = jnp.where((y + c + bit(FLIP_ODD, k)) % 2 == 0, 1, 3)
    even = jnp.where((y + c + bit(FLIP_EVEN, k)) % 2 == 0, 0, 2)
    x = (k + jnp.where(y < 2, odd, even)) % 4
    return (c + bit(FLIP_Z, k)) % 2 * 8 + x * 2 + (low + bit(FLIP_CORE, k)) % 2


def slot_of(s, k):
    c = (s // 8 + bit(FLIP_Z, k)) % 2
    low = (s % 2 + bit(FLIP_CORE, k)) % 2
    move = (s // 2 + 8 - k) % 4
    odd = (jnp.where(move == 3, 1, 0) + c + bit(FLIP_ODD, k)) % 2
    even = 2 + (jnp.where(move == 2, 1, 0) + c + bit(FLIP_EVEN, k)) % 2
    return c * 8 + jnp.where(move % 2 == 1, odd, even) * 2 + low


def held(s, k):
    slot = slot_of(s, k)
    return 2 * k + slot // 8, slot % 8


def project(
    hv, w, given, q_out, kv_out, kx, vt, code, meta,
    wk, wq, kvs, qs, load, a2a_s, a2a_r, q_s, q_r, g_s, g_r, loc,
):
    s, j = lax.axis_index("seq"), lax.axis_index("head")
    zh, x, c = s // 8, (s // 2) % 4, s % 2
    to = dealt(s, j)
    mine = to == s

    loads = []
    for r in range(8):
        g = lax.rem(j + r + 1, 8)
        col = pl.multiple_of(g * COLS + QPK * HD, 128)
        loads.append(pltpu.make_async_copy(w.at[:, pl.ds(col, 2 * HD)], wk.at[r], load.at[r]))
        loads[-1].start()
    for r in range(8):
        g = lax.rem(j + r + 1, 8)
        col = pl.multiple_of(g * COLS, 128)
        loads.append(pltpu.make_async_copy(w.at[:, pl.ds(col, QPK * HD)], wq.at[r], load.at[8 + r]))

    def block(zz, xx, cc):
        return zz * 8 + xx * 2 + cc

    right, left = lax.rem(x + 1, 4), lax.rem(x + 3, 4)
    far = lax.rem(x + 2, 4)
    peers = [(block(zh, right, c), j), (block(zh, left, c), j), (block(1 - zh, x, c), j), (block(zh, x, 1 - c), j)]

    barrier = pltpu.get_barrier_semaphore()
    for p in peers:
        pl.semaphore_signal(barrier, inc=1, device_id=p, device_id_type=MESH)
    for r in range(7):
        pl.semaphore_signal(barrier, inc=1, device_id=(s, lax.rem(j + r + 1, 8)), device_id_type=MESH)
    for k in range(STRIPES):
        own = mine & (s // 2 == k)

        @pl.when(jnp.logical_not(own))
        def _():
            pl.semaphore_signal(barrier, inc=1, device_id=held(s, k), device_id_type=MESH)

    down = lax.broadcasted_iota(jnp.int32, (128, 128), 0)
    along = lax.broadcasted_iota(jnp.int32, (128, 128), 1)
    pick = (along[:HD] == down[:HD] + HD).astype(bf16)
    marks = (down >= HD) & (down < HD + SEGS)
    mark_row = (along[:1] >= HD) & (along[:1] < HD + SEGS)

    def tables():
        code[...] = given[...] & 31
        seg = code[...] & 15
        lane = along[:1]
        for k in range(STRIPES):
            stripe = 16 * k + slot_of(s, k)
            own = code[pl.ds(stripe, 1), :][:, :1] & 15
            before = jnp.where(seg < own, 1.0, 0.0)
            begin = jnp.sum(jnp.sum(before, axis=0, keepdims=True), axis=1, keepdims=True).astype(jnp.int32)
            blocks = lax.shift_right_logical(stripe * ROWS - begin + BK - 1, BK.bit_length() - 1)
            meta[k : k + 1, :] = jnp.where(lane == 0, blocks, own)
        at = jnp.zeros((64, 128), f32)
        for n in range(TOKENS // PAGE // 128):
            hit = lax.shift_right_logical(given[n : n + 1, :], 5) == 64 * s + down[:64]
            at += jnp.where(hit, (n * 128 + along[:64]).astype(f32), 0.0)
        logical = jnp.sum(at, axis=1, keepdims=True).astype(jnp.int32)
        meta[STRIPES:, :] = jnp.broadcast_to(logical, (64, 128))
        kx[:PAD] = jnp.broadcast_to(jnp.where(mark_row, NEG, 0.0), (PAD, 2 * HD)).astype(bf16)
        vt[:HD, :PAD] = jnp.zeros((HD, PAD), bf16)
        vt[HD:, :] = jnp.ones((VR - HD, PAD + TOKENS), bf16)

    def use(b, h):
        at = pl.multiple_of(b * GT + h * CH, 128)
        to = pl.multiple_of(PAD + at, 128)
        rows = kv_out[pl.ds(at, CH), :]
        vt[:HD, pl.ds(to, CH)] = lax.dot_general(pick, rows, NT, preferred_element_type=f32).astype(bf16)
        for n in range(CH // 128):
            row = code[pl.ds(b * (GT // 128) + h * (CH // 128) + n, 1), :]
            mark = jnp.where(marks & (row != down - HD), NEG, 0.0).T.astype(bf16)
            kx[pl.ds(to + n * 128, 128), :] = jnp.where(along[:1] < HD, rows[n * 128 : (n + 1) * 128], mark)

    def query(r):
        loads[8 + r].wait()
        qs[r] = (jnp.dot(hv[...], wq[r], preferred_element_type=f32).astype(bf16) * 0.015625).astype(bf16)

    row0 = pl.multiple_of(s * GT + j * ROWS, ROWS)
    sends = []

    def send_keys(r):
        cp = pltpu.make_async_remote_copy(
            src_ref=kvs.at[r],
            dst_ref=kv_out.at[pl.ds(row0, ROWS)],
            send_sem=a2a_s.at[r],
            recv_sem=a2a_r.at[r],
            device_id=(s, lax.rem(j + r + 1, 8)),
            device_id_type=MESH,
        )
        cp.start()
        sends.append(cp)

    for r in range(8):
        loads[r].wait()
        if r == FIRST:
            for n in range(8):
                loads[8 + n].start()
        kvs[r] = jnp.dot(hv[...], wk[r], preferred_element_type=f32).astype(bf16)
        if r == FIRST:
            pl.semaphore_wait(barrier, jnp.where(mine, 18, 19))
            for n in range(r + 1):
                send_keys(n)
        elif FIRST < r < 7:
            send_keys(r)
    own_kv = pltpu.make_async_copy(kvs.at[7], kv_out.at[pl.ds(row0, ROWS)], loc)
    own_kv.start()

    R, L, Z, C = range(4)
    held_at = {}

    def half(b, h):
        return kv_out.at[pl.ds(pl.multiple_of(held_at[b] * GT + h * CH, 128), CH)]

    copies = {}

    def pass_on(b, h, *to_peers):
        for peer in to_peers:
            i = len(copies)
            copies[b, h, peer] = i
            cp = pltpu.make_async_remote_copy(
                src_ref=half(b, h),
                dst_ref=half(b, h),
                send_sem=g_s.at[i],
                recv_sem=g_r.at[i],
                device_id=peers[peer],
                device_id_type=MESH,
            )
            cp.start()
            sends.append(cp)

    def arrived(b, h, sent, peer):
        pltpu.make_async_copy(half(b, h), half(b, h), g_r.at[copies[sent, h, peer]]).wait()

    slot = s // 2
    qsends = []

    def send_query(r):
        cp = pltpu.make_async_remote_copy(
            src_ref=qs.at[r],
            dst_ref=q_out.at[slot],
            send_sem=q_s.at[r],
            recv_sem=q_r.at[slot],
            device_id=(to, lax.rem(j + r + 1, 8)),
            device_id_type=MESH,
        )
        qsends.append(cp)
        if r < 7:
            cp.start()
        else:

            @pl.when(jnp.logical_not(mine))
            def _():
                cp.start()

            @pl.when(mine)
            def _():
                pltpu.make_async_copy(qs.at[7], q_out.at[slot], q_r.at[slot]).start()

    for r in range(8):
        query(r)
        send_query(r)
    tables()
    own_kv.wait()
    for r in range(7):
        source = lax.rem(j + 7 - r, 8)
        there = kv_out.at[pl.ds(pl.multiple_of(s * GT + source * ROWS, ROWS), ROWS)]
        pltpu.make_async_copy(there, there, a2a_r.at[r]).wait()
    places = (("m", x), ("l", left), ("r", right), ("f", far))
    for half_z, zz in (("o", zh), ("z", 1 - zh)):
        for core, cc in (("", c), ("c", 1 - c)):
            for name, xx in places:
                held_at[half_z + name + core] = block(zz, xx, cc)
    low, high = range(CHUNKS // 2), range(CHUNKS // 2, CHUNKS)
    for h in low:
        pass_on("om", h, R, Z)
    for h in high:
        pass_on("om", h, L, Z)
    for h in high:
        pass_on("om", h, R)
    for h in low:
        pass_on("om", h, L, C)
    for h in high:
        pass_on("om", h, C)

    def ready(b, *chunks):
        for h in chunks:
            use(held_at[b], h)

    def other(b, *chunks):
        for h in chunks:
            arrived(b + "c", h, b, C)
            use(held_at[b + "c"], h)

    for h, g in zip(low, high, strict=True):
        arrived("ol", h, "om", R)
        pass_on("ol", h, R, C)
        arrived("or", g, "om", L)
        pass_on("or", g, L, C)
        ready("om", h)
    for h in (*low, *high):
        arrived("zm", h, "om", Z)
        pass_on("zm", h, R, L, C)
        if h in high:
            ready("om", h)
    for h, g in zip(low, high, strict=True):
        arrived("ol", g, "om", R)
        pass_on("ol", g, C)
        arrived("or", h, "om", L)
        pass_on("or", h, C)
        ready("ol", h)
        ready("or", g)
    for h, g in zip(low, high, strict=True):
        arrived("of", h, "ol", R)
        pass_on("of", h, Z, C)
        arrived("of", g, "or", L)
        pass_on("of", g, Z, C)
        ready("zm", h, g)
        other("om", h, g)
    ready("ol", *high)
    ready("or", *low)
    other("ol", *low)
    other("or", *high)
    other("zm", *low)
    for h in (*low, *high):
        arrived("zl", h, "zm", R)
        pass_on("zl", h, C)
        arrived("zr", h, "zm", L)
        pass_on("zr", h, C)
        if h in low:
            other("zm", h + CHUNKS // 2)
            other("ol", h + CHUNKS // 2)
            other("or", h)
        else:
            ready("of", h - CHUNKS // 2, h)
            other("of", h - CHUNKS // 2, h)
            ready("zl", h - CHUNKS // 2)
            ready("zr", h - CHUNKS // 2)
    ready("zl", *high)
    ready("zr", *high)
    for h, g in zip(low, high, strict=True):
        arrived("zf", h, "of", Z)
        pass_on("zf", h, C)
        other("zl", h)
        other("zr", h)
        arrived("zf", g, "of", Z)
        pass_on("zf", g, C)
    other("zl", *high)
    other("zr", *high)
    ready("zf", *low, *high)
    other("zf", *low, *high)

    for k in range(STRIPES):
        pltpu.make_async_copy(q_out.at[k], q_out.at[k], q_r.at[k]).wait()
    for cp in sends + qsends[:7]:
        cp.wait_send()

    @pl.when(jnp.logical_not(mine))
    def _():
        qsends[7].wait_send()


BATCH = 8


def attend(meta_in, code, q, kv, kx, vt, att, pool, meta, item_k, item_at, qt, m, acc, sa, sb, sem, page_sem):
    s = lax.axis_index("seq")
    fetch = pltpu.make_async_copy(meta_in, meta, sem)
    fetch.start()
    down = lax.broadcasted_iota(jnp.int32, (128, 128), 0)
    along = lax.broadcasted_iota(jnp.int32, (128, 128), 1)
    wide = QPK * ROWS
    fetch.wait()

    def place(k):
        return pl.multiple_of(PAD + (16 * k + slot_of(s, k)) * ROWS, 128)

    def stripe_items(k, n):
        here = place(k)

        def one(b, n):
            item_k[n] = k
            item_at[n] = here - (b + 1) * BK
            return n + 1

        return lax.fori_loop(0, meta[k, 0], one, n)

    total = lax.fori_loop(0, STRIPES, stripe_items, 0)
    for n in range(3):
        item_k[total + n] = STRIPES - 1
        item_at[total + n] = 0

    def peak(sc):
        return jnp.max(sc.reshape(sc.shape[0] // 8, 8, sc.shape[1]), axis=0)

    @pl.loop(0, STRIPES // BATCH)
    def _(group):
        for n in range(64 * BATCH // STRIPES):
            i = group * (64 * BATCH // STRIPES) + n
            at = pl.multiple_of(meta[STRIPES + i, 0] * PAGE, PAGE)
            to = pl.multiple_of(i * PAGE, PAGE)
            pltpu.make_async_copy(kv.at[pl.ds(at, PAGE)], pool.at[pl.ds(to, PAGE)], page_sem).start()
        parts, same = [], []
        for n in range(BATCH):
            k = group * BATCH + n
            own = meta[k, 1]
            here = place(k)
            tq = [q[k, :, c * HD : (c + 2) * HD].T for c in range(0, QPK, 2)]
            tq = jnp.concatenate([h for t in tq for h in (t[:HD], t[HD:])], axis=1)
            qt[k, :HD, :] = tq
            qt[k, HD:, :] = (lax.broadcasted_iota(jnp.int32, (HD, wide), 0) == own).astype(bf16)
            row = code[pl.ds((here - PAD) // 128, 1), :]
            ct = jnp.broadcast_to(row, (ROWS, ROWS))
            cu = ct.T
            allowed = ((cu & 15) == (ct & 15)) & (down <= along) & ((cu < 16) | (down == along))
            sc = jnp.dot(kx[pl.ds(here, ROWS), :HD], tq, preferred_element_type=f32)
            parts += [jnp.where(allowed, sc[:, c * ROWS : (c + 1) * ROWS], NEG) for c in range(QPK)]
            same += [(row & 15) == own] * QPK
        sc = jnp.concatenate(parts, axis=1)
        top = jnp.max(peak(sc), axis=0, keepdims=True)
        p = jnp.exp(sc - top).astype(bf16)
        start = jnp.where(jnp.concatenate(same, axis=1), top, -NEG)
        for n in range(BATCH):
            k = group * BATCH + n
            cols = slice(n * wide, (n + 1) * wide)
            acc[k] = jnp.dot(vt[:, pl.ds(place(k), ROWS)], p[:, cols], preferred_element_type=f32)
            m[k] = start[:, cols]

    def scores(n):
        keys = kx[pl.ds(pl.multiple_of(item_at[n], 128), BK), :]
        return jnp.dot(keys, qt[item_k[n]], preferred_element_type=f32)

    def weigh(n, src, dst, peaks):
        k = item_k[n]
        old = m[k]
        top = jnp.maximum(old, jnp.max(peaks, axis=0, keepdims=True))
        m[k] = top
        sc = scores(n + 1)
        dst[...] = sc
        p = jnp.exp(src[...] - top).astype(bf16)
        part = jnp.dot(vt[:, pl.ds(pl.multiple_of(item_at[n], 128), BK)], p, preferred_element_type=f32)
        acc[k] = acc[k] * jnp.exp(old - top) + part
        return peak(sc)

    def pair(i, peaks):
        peaks = weigh(2 * i, sa, sb, peaks)
        return weigh(2 * i + 1, sb, sa, peaks)

    sc = scores(0)
    sa[...] = sc
    lax.fori_loop(0, (total + 1) // 2, pair, peak(sc))

    @pl.loop(0, STRIPES // BATCH)
    def _(group):
        for n in range(BATCH):
            k = group * BATCH + n
            done = acc[k, :HD, :] / acc[k, HD : HD + 1, :]
            for c in range(0, QPK, 2):
                two = [done[:, (c + d) * ROWS : (c + d + 1) * ROWS] for d in range(2)]
                att[k, :, c * HD : (c + 2) * HD] = jnp.concatenate(two, axis=0).T.astype(bf16)

    pltpu.make_async_copy(kv.at[pl.ds(0, GT)], pool, page_sem).wait()


def mix(att, w, out, got, acc, a_s, a_r):
    s, j = lax.axis_index("seq"), lax.axis_index("head")
    to = dealt(s, j)
    mine = to == s
    barrier = pltpu.get_barrier_semaphore()
    for r in range(8):
        h = lax.rem(j + r + 1, 8)
        if r < 7:
            pl.semaphore_signal(barrier, inc=1, device_id=(to, h), device_id_type=MESH)
        else:

            @pl.when(jnp.logical_not(mine))
            def _():
                pl.semaphore_signal(barrier, inc=1, device_id=(to, h), device_id_type=MESH)

    pl.semaphore_wait(barrier, jnp.where(mine, 7, 8))

    copies = []
    for r in range(STRIPES):
        k = lax.rem(s // 2 + j + r, STRIPES)
        own = mine & (s // 2 == k)
        cp = pltpu.make_async_remote_copy(
            src_ref=att.at[k],
            dst_ref=got.at[j],
            send_sem=a_s.at[k],
            recv_sem=a_r.at[j],
            device_id=held(s, k),
            device_id_type=MESH,
        )
        copies.append((own, cp))

        @pl.when(jnp.logical_not(own))
        def _():
            cp.start()

        @pl.when(own)
        def _():
            pltpu.make_async_copy(att.at[k], got.at[j], a_r.at[j]).start()

    for r in range(8):
        h = lax.rem(j + 8 - r, 8)
        pltpu.make_async_copy(got.at[h], got.at[h], a_r.at[h]).wait()
        part = jnp.dot(
            got[h], w[pl.ds(pl.multiple_of(h * QPK * HD, QPK * HD), QPK * HD), :], preferred_element_type=f32
        )
        if r == 0:
            acc[...] = part
        elif r < 7:
            acc[...] += part
        else:
            out[...] = (acc[...] + part).astype(bf16)
    for own, cp in copies:

        @pl.when(jnp.logical_not(own))
        def _():
            cp.wait_send()


ANY = pl.BlockSpec(memory_space=pl.ANY)
SMEM = pl.BlockSpec(memory_space=pltpu.SMEM)
VMEM = pl.BlockSpec(memory_space=pltpu.VMEM)
DMA = pltpu.SemaphoreType.DMA


HBM = pl.BlockSpec(memory_space=pltpu.HBM)


def projected(hidden, w_qkv, given):
    return pl.pallas_call(
        project,
        out_shape=(
            jax.ShapeDtypeStruct((STRIPES, ROWS, QPK * HD), bf16),
            jax.ShapeDtypeStruct((TOKENS, 2 * HD), bf16),
            jax.ShapeDtypeStruct((PAD + TOKENS, 2 * HD), bf16),
            jax.ShapeDtypeStruct((VR, PAD + TOKENS), bf16),
            jax.ShapeDtypeStruct((TOKENS // 128, 128), jnp.int32),
            jax.ShapeDtypeStruct((META, 128), jnp.int32),
        ),
        in_specs=[VMEM, HBM, VMEM],
        out_specs=(VMEM,) * 6,
        scratch_shapes=[
            pltpu.VMEM((KVH, D, 2 * HD), bf16),
            pltpu.VMEM((KVH, D, QPK * HD), bf16),
            pltpu.VMEM((KVH, ROWS, 2 * HD), bf16),
            pltpu.VMEM((KVH, ROWS, QPK * HD), bf16),
            DMA((16,)),
            DMA((7,)),
            DMA((7,)),
            DMA((8,)),
            DMA((8,)),
            DMA((15 * CHUNKS,)),
            DMA((15 * CHUNKS,)),
            DMA,
        ],
        compiler_params=pltpu.CompilerParams(collective_id=0, has_side_effects=True, vmem_limit_bytes=34 << 20),
        name="project",
    )(hidden, w_qkv, given)


def shards(hidden, w_qkv, w_out, seg_ids, live, page_table):
    pages = jnp.pad(page_table, (0, TOKENS - TOKENS // PAGE))
    given = (seg_ids + 16 * (1 - live) + 32 * pages).reshape(-1, 128)
    q, kv, kx, vt, code, meta = projected(hidden, w_qkv, given)
    att, pool = pl.pallas_call(
        attend,
        out_shape=(
            jax.ShapeDtypeStruct((STRIPES, ROWS, QPK * HD), bf16),
            jax.ShapeDtypeStruct((GT, 2 * HD), bf16),
        ),
        in_specs=[ANY, VMEM, VMEM, VMEM, VMEM, VMEM],
        out_specs=(VMEM, HBM),
        scratch_shapes=[
            pltpu.SMEM((META, 128), jnp.int32),
            pltpu.SMEM((ITEMS,), jnp.int32),
            pltpu.SMEM((ITEMS,), jnp.int32),
            pltpu.VMEM((STRIPES, 2 * HD, QPK * ROWS), bf16),
            pltpu.VMEM((STRIPES, 1, QPK * ROWS), f32),
            pltpu.VMEM((STRIPES, VR, QPK * ROWS), f32),
            pltpu.VMEM((BK, QPK * ROWS), f32),
            pltpu.VMEM((BK, QPK * ROWS), f32),
            DMA,
            DMA,
        ],
        compiler_params=pltpu.CompilerParams(vmem_limit_bytes=20 << 20),
        name="attend",
    )(meta, code, q, kv, kx, vt)

    mixed = pl.pallas_call(
        mix,
        out_shape=jax.ShapeDtypeStruct((ROWS, D), bf16),
        in_specs=[ANY, VMEM],
        out_specs=VMEM,
        scratch_shapes=[
            pltpu.VMEM((KVH, ROWS, QPK * HD), bf16),
            pltpu.VMEM((ROWS, D), f32),
            DMA((8,)),
            DMA((8,)),
        ],
        compiler_params=pltpu.CompilerParams(collective_id=1, has_side_effects=True, vmem_limit_bytes=12 << 20),
        name="mix",
    )(att, w_out)
    return mixed, pool.reshape(1, TOKENS // PAGE // SEQ, PAGE, 2 * HD)


def solution(mesh):
    placed = (P(("seq", "head"), None), P(), P(), P(), P(), P())
    return jax.shard_map(
        shards,
        mesh=mesh,
        in_specs=placed,
        out_specs=(P(("seq", "head"), None), P("head", "seq", None, None)),
        check_vma=False,
    )
```

```python
import functools

import jax
import jax.numpy as jnp
from jax import lax
from jax.experimental import pallas as pl
from jax.experimental.pallas import tpu as pltpu
from jax.sharding import PartitionSpec as P

D = 2048
TOKENS = 16384
KVH = 8
HD = 64
QPK = 4
PAGE = 16
SEQ = 16
SEGS = 8
ROWS = 128
GT = 1024
COLS = (QPK + 2) * HD
STRIPES = 8
BK = 640
PAD = 2 * BK
ITEMS = STRIPES * (TOKENS // BK) + 8
META = STRIPES + 64
CHUNKS = 2
CH = GT // CHUNKS
FIRST = 3
NEG = -1e30
MESH = pl.DeviceIdType.MESH
bf16, f32 = jnp.bfloat16, jnp.float32


FLIP_Z = (1, 0, 0, 1, 1, 0, 0, 0)
FLIP_CORE = (0, 1, 1, 0, 1, 0, 1, 0)
FLIP_ODD = (1, 1, 1, 0, 0, 0, 0, 0)
FLIP_EVEN = (0, 0, 1, 0, 0, 1, 1, 1)


def bit(table, k):
    if isinstance(k, int):
        return table[k]
    return sum(jnp.where(k == n, 1, 0) for n in range(8) if table[n])


NT = (((1,), (1,)), ((), ()))
VR = HD + 16


def dealt(s, j):
    k, c, y, low = s // 2, s % 2, j // 2, j % 2
    odd = jnp.where((y + c + bit(FLIP_ODD, k)) % 2 == 0, 1, 3)
    even = jnp.where((y + c + bit(FLIP_EVEN, k)) % 2 == 0, 0, 2)
    x = (k + jnp.where(y < 2, odd, even)) % 4
    return (c + bit(FLIP_Z, k)) % 2 * 8 + x * 2 + (low + bit(FLIP_CORE, k)) % 2


def slot_of(s, k):
    c = (s // 8 + bit(FLIP_Z, k)) % 2
    low = (s % 2 + bit(FLIP_CORE, k)) % 2
    move = (s // 2 + 8 - k) % 4
    odd = (jnp.where(move == 3, 1, 0) + c + bit(FLIP_ODD, k)) % 2
    even = 2 + (jnp.where(move == 2, 1, 0) + c + bit(FLIP_EVEN, k)) % 2
    return c * 8 + jnp.where(move % 2 == 1, odd, even) * 2 + low


def held(s, k):
    slot = slot_of(s, k)
    return 2 * k + slot // 8, slot % 8


def project(
    hv, w, given, q_out, kv_out, kx, vt, code, meta,
    wk, wq, kvs, qs, load, a2a_s, a2a_r, q_s, q_r, g_s, g_r, loc,
):
    s, j = lax.axis_index("seq"), lax.axis_index("head")
    zh, x, c = s // 8, (s // 2) % 4, s % 2
    to = dealt(s, j)
    mine = to == s

    loads = []
    for r in range(8):
        g = lax.rem(j + r + 1, 8)
        col = pl.multiple_of(g * COLS + QPK * HD, 128)
        loads.append(pltpu.make_async_copy(w.at[:, pl.ds(col, 2 * HD)], wk.at[r], load.at[r]))
        loads[-1].start()
    for r in range(8):
        g = lax.rem(j + r + 1, 8)
        col = pl.multiple_of(g * COLS, 128)
        loads.append(pltpu.make_async_copy(w.at[:, pl.ds(col, QPK * HD)], wq.at[r], load.at[8 + r]))

    def block(zz, xx, cc):
        return zz * 8 + xx * 2 + cc

    right, left = lax.rem(x + 1, 4), lax.rem(x + 3, 4)
    far = lax.rem(x + 2, 4)
    peers = [(block(zh, right, c), j), (block(zh, left, c), j), (block(1 - zh, x, c), j), (block(zh, x, 1 - c), j)]

    barrier = pltpu.get_barrier_semaphore()
    for p in peers:
        pl.semaphore_signal(barrier, inc=1, device_id=p, device_id_type=MESH)
    for r in range(7):
        pl.semaphore_signal(barrier, inc=1, device_id=(s, lax.rem(j + r + 1, 8)), device_id_type=MESH)
    for k in range(STRIPES):
        own = mine & (s // 2 == k)

        @pl.when(jnp.logical_not(own))
        def _():
            pl.semaphore_signal(barrier, inc=1, device_id=held(s, k), device_id_type=MESH)

    down = lax.broadcasted_iota(jnp.int32, (128, 128), 0)
    along = lax.broadcasted_iota(jnp.int32, (128, 128), 1)
    pick = (along[:HD] == down[:HD] + HD).astype(bf16)
    marks = (down >= HD) & (down < HD + SEGS)
    mark_row = (along[:1] >= HD) & (along[:1] < HD + SEGS)

    def tables():
        code[...] = given[...] & 31
        seg = code[...] & 15
        lane = along[:1]
        for k in range(STRIPES):
            stripe = 16 * k + slot_of(s, k)
            own = code[pl.ds(stripe, 1), :][:, :1] & 15
            before = jnp.where(seg < own, 1.0, 0.0)
            begin = jnp.sum(jnp.sum(before, axis=0, keepdims=True), axis=1, keepdims=True).astype(jnp.int32)
            blocks = ((stripe * ROWS - begin + BK - 1).astype(f32) + 0.5) * (1.0 / BK)
            blocks = blocks.astype(jnp.int32)
            meta[k : k + 1, :] = jnp.where(lane == 0, blocks, own)
        at = jnp.zeros((64, 128), f32)
        for n in range(TOKENS // PAGE // 128):
            hit = lax.shift_right_logical(given[n : n + 1, :], 5) == 64 * s + down[:64]
            at += jnp.where(hit, (n * 128 + along[:64]).astype(f32), 0.0)
        logical = jnp.sum(at, axis=1, keepdims=True).astype(jnp.int32)
        meta[STRIPES:, :] = jnp.broadcast_to(logical, (64, 128))
        kx[:PAD] = jnp.broadcast_to(jnp.where(mark_row, NEG, 0.0), (PAD, 2 * HD)).astype(bf16)
        vt[:HD, :PAD] = jnp.zeros((HD, PAD), bf16)
        vt[HD:, :] = jnp.ones((VR - HD, PAD + TOKENS), bf16)

    def use(b, h):
        at = pl.multiple_of(b * GT + h * CH, 128)
        to = pl.multiple_of(PAD + at, 128)
        rows = kv_out[pl.ds(at, CH), :]
        vt[:HD, pl.ds(to, CH)] = lax.dot_general(pick, rows, NT, preferred_element_type=f32).astype(bf16)
        for n in range(CH // 128):
            row = code[pl.ds(b * (GT // 128) + h * (CH // 128) + n, 1), :]
            mark = jnp.where(marks & (row != down - HD), NEG, 0.0).T.astype(bf16)
            kx[pl.ds(to + n * 128, 128), :] = jnp.where(along[:1] < HD, rows[n * 128 : (n + 1) * 128], mark)

    def query(r):
        loads[8 + r].wait()
        qs[r] = (jnp.dot(hv[...], wq[r], preferred_element_type=f32).astype(bf16) * 0.015625).astype(bf16)

    row0 = pl.multiple_of(s * GT + j * ROWS, ROWS)
    sends = []

    def send_keys(r):
        cp = pltpu.make_async_remote_copy(
            src_ref=kvs.at[r],
            dst_ref=kv_out.at[pl.ds(row0, ROWS)],
            send_sem=a2a_s.at[r],
            recv_sem=a2a_r.at[r],
            device_id=(s, lax.rem(j + r + 1, 8)),
            device_id_type=MESH,
        )
        cp.start()
        sends.append(cp)

    for r in range(8):
        loads[r].wait()
        if r == FIRST:
            for n in range(8):
                loads[8 + n].start()
        kvs[r] = jnp.dot(hv[...], wk[r], preferred_element_type=f32).astype(bf16)
        if r == FIRST:
            pl.semaphore_wait(barrier, jnp.where(mine, 18, 19))
            for n in range(r + 1):
                send_keys(n)
        elif FIRST < r < 7:
            send_keys(r)
    own_kv = pltpu.make_async_copy(kvs.at[7], kv_out.at[pl.ds(row0, ROWS)], loc)
    own_kv.start()

    R, L, Z, C = range(4)
    held_at = {}

    def half(b, h):
        return kv_out.at[pl.ds(pl.multiple_of(held_at[b] * GT + h * CH, 128), CH)]

    copies = {}

    def pass_on(b, h, *to_peers):
        for peer in to_peers:
            i = len(copies)
            copies[b, h, peer] = i
            cp = pltpu.make_async_remote_copy(
                src_ref=half(b, h),
                dst_ref=half(b, h),
                send_sem=g_s.at[i],
                recv_sem=g_r.at[i],
                device_id=peers[peer],
                device_id_type=MESH,
            )
            cp.start()
            sends.append(cp)

    def arrived(b, h, sent, peer):
        pltpu.make_async_copy(half(b, h), half(b, h), g_r.at[copies[sent, h, peer]]).wait()

    slot = s // 2
    qsends = []

    def send_query(r):
        cp = pltpu.make_async_remote_copy(
            src_ref=qs.at[r],
            dst_ref=q_out.at[slot],
            send_sem=q_s.at[r],
            recv_sem=q_r.at[slot],
            device_id=(to, lax.rem(j + r + 1, 8)),
            device_id_type=MESH,
        )
        qsends.append(cp)
        if r < 7:
            cp.start()
        else:

            @pl.when(jnp.logical_not(mine))
            def _():
                cp.start()

            @pl.when(mine)
            def _():
                pltpu.make_async_copy(qs.at[7], q_out.at[slot], q_r.at[slot]).start()

    for r in range(8):
        query(r)
        send_query(r)
    tables()
    own_kv.wait()
    for r in range(7):
        source = lax.rem(j + 7 - r, 8)
        there = kv_out.at[pl.ds(pl.multiple_of(s * GT + source * ROWS, ROWS), ROWS)]
        pltpu.make_async_copy(there, there, a2a_r.at[r]).wait()
    places = (("m", x), ("l", left), ("r", right), ("f", far))
    for half_z, zz in (("o", zh), ("z", 1 - zh)):
        for core, cc in (("", c), ("c", 1 - c)):
            for name, xx in places:
                held_at[half_z + name + core] = block(zz, xx, cc)
    low, high = range(CHUNKS // 2), range(CHUNKS // 2, CHUNKS)
    for h in low:
        pass_on("om", h, R, Z)
    for h in high:
        pass_on("om", h, L, Z)
    for h in high:
        pass_on("om", h, R)
    for h in low:
        pass_on("om", h, L, C)
    for h in high:
        pass_on("om", h, C)

    def ready(b, *chunks):
        for h in chunks:
            use(held_at[b], h)

    def other(b, *chunks):
        for h in chunks:
            arrived(b + "c", h, b, C)
            use(held_at[b + "c"], h)

    for h, g in zip(low, high, strict=True):
        arrived("ol", h, "om", R)
        pass_on("ol", h, R, C)
        arrived("or", g, "om", L)
        pass_on("or", g, L, C)
        ready("om", h)
    for h in (*low, *high):
        arrived("zm", h, "om", Z)
        pass_on("zm", h, R, L, C)
        if h in high:
            ready("om", h)
    for h, g in zip(low, high, strict=True):
        arrived("ol", g, "om", R)
        pass_on("ol", g, C)
        arrived("or", h, "om", L)
        pass_on("or", h, C)
        ready("ol", h)
        ready("or", g)
    for h, g in zip(low, high, strict=True):
        arrived("of", h, "ol", R)
        pass_on("of", h, Z, C)
        arrived("of", g, "or", L)
        pass_on("of", g, Z, C)
        ready("zm", h, g)
        other("om", h, g)
    ready("ol", *high)
    ready("or", *low)
    other("ol", *low)
    other("or", *high)
    other("zm", *low)
    for h in (*low, *high):
        arrived("zl", h, "zm", R)
        pass_on("zl", h, C)
        arrived("zr", h, "zm", L)
        pass_on("zr", h, C)
        if h in low:
            other("zm", h + CHUNKS // 2)
            other("ol", h + CHUNKS // 2)
            other("or", h)
        else:
            ready("of", h - CHUNKS // 2, h)
            other("of", h - CHUNKS // 2, h)
            ready("zl", h - CHUNKS // 2)
            ready("zr", h - CHUNKS // 2)
    ready("zl", *high)
    ready("zr", *high)
    for h, g in zip(low, high, strict=True):
        arrived("zf", h, "of", Z)
        pass_on("zf", h, C)
        other("zl", h)
        other("zr", h)
        arrived("zf", g, "of", Z)
        pass_on("zf", g, C)
    other("zl", *high)
    other("zr", *high)
    ready("zf", *low, *high)
    other("zf", *low, *high)

    for k in range(STRIPES):
        pltpu.make_async_copy(q_out.at[k], q_out.at[k], q_r.at[k]).wait()
    for cp in sends + qsends[:7]:
        cp.wait_send()

    @pl.when(jnp.logical_not(mine))
    def _():
        qsends[7].wait_send()


BATCH = 8


def attend(meta_in, code, q, kv, kx, vt, att, pool, meta, item_k, item_at, qt, m, acc, sa, sb, sem, page_sem):
    s = lax.axis_index("seq")
    fetch = pltpu.make_async_copy(meta_in, meta, sem)
    fetch.start()
    down = lax.broadcasted_iota(jnp.int32, (128, 128), 0)
    along = lax.broadcasted_iota(jnp.int32, (128, 128), 1)
    wide = QPK * ROWS
    fetch.wait()

    def place(k):
        return pl.multiple_of(PAD + (16 * k + slot_of(s, k)) * ROWS, 128)

    def stripe_items(k, n):
        here = place(k)

        def one(b, n):
            item_k[n] = k
            item_at[n] = here - (b + 1) * BK
            return n + 1

        return lax.fori_loop(0, meta[k, 0], one, n)

    total = lax.fori_loop(0, STRIPES, stripe_items, 0)
    for n in range(3):
        item_k[total + n] = STRIPES - 1
        item_at[total + n] = 0

    def peak(sc):
        return jnp.max(sc.reshape(sc.shape[0] // 8, 8, sc.shape[1]), axis=0)

    @pl.loop(0, STRIPES // BATCH)
    def _(group):
        for n in range(64 * BATCH // STRIPES):
            i = group * (64 * BATCH // STRIPES) + n
            at = pl.multiple_of(meta[STRIPES + i, 0] * PAGE, PAGE)
            to = pl.multiple_of(i * PAGE, PAGE)
            pltpu.make_async_copy(kv.at[pl.ds(at, PAGE)], pool.at[pl.ds(to, PAGE)], page_sem).start()
        parts, same = [], []
        for n in range(BATCH):
            k = group * BATCH + n
            own = meta[k, 1]
            here = place(k)
            tq = [q[k, :, c * HD : (c + 2) * HD].T for c in range(0, QPK, 2)]
            tq = jnp.concatenate([h for t in tq for h in (t[:HD], t[HD:])], axis=1)
            qt[k, :HD, :] = tq
            qt[k, HD:, :] = (lax.broadcasted_iota(jnp.int32, (HD, wide), 0) == own).astype(bf16)
            row = code[pl.ds((here - PAD) // 128, 1), :]
            ct = jnp.broadcast_to(row, (ROWS, ROWS))
            cu = ct.T
            allowed = ((cu & 15) == (ct & 15)) & (down <= along) & ((cu < 16) | (down == along))
            sc = jnp.dot(kx[pl.ds(here, ROWS), :HD], tq, preferred_element_type=f32)
            parts += [jnp.where(allowed, sc[:, c * ROWS : (c + 1) * ROWS], NEG) for c in range(QPK)]
            same += [(row & 15) == own] * QPK
        sc = jnp.concatenate(parts, axis=1)
        top = jnp.max(peak(sc), axis=0, keepdims=True)
        p = jnp.exp(sc - top).astype(bf16)
        start = jnp.where(jnp.concatenate(same, axis=1), top, -NEG)
        for n in range(BATCH):
            k = group * BATCH + n
            cols = slice(n * wide, (n + 1) * wide)
            acc[k] = jnp.dot(vt[:, pl.ds(place(k), ROWS)], p[:, cols], preferred_element_type=f32)
            m[k] = start[:, cols]

    def scores(n):
        keys = kx[pl.ds(pl.multiple_of(item_at[n], 128), BK), :]
        return jnp.dot(keys, qt[item_k[n]], preferred_element_type=f32)

    def weigh(n, src, dst, peaks):
        k = item_k[n]
        old = m[k]
        top = jnp.maximum(old, jnp.max(peaks, axis=0, keepdims=True))
        m[k] = top
        sc = scores(n + 1)
        dst[...] = sc
        p = jnp.exp(src[...] - top).astype(bf16)
        part = jnp.dot(vt[:, pl.ds(pl.multiple_of(item_at[n], 128), BK)], p, preferred_element_type=f32)
        acc[k] = acc[k] * jnp.exp(old - top) + part
        return peak(sc)

    def pair(i, peaks):
        peaks = weigh(2 * i, sa, sb, peaks)
        return weigh(2 * i + 1, sb, sa, peaks)

    sc = scores(0)
    sa[...] = sc
    lax.fori_loop(0, (total + 1) // 2, pair, peak(sc))

    @pl.loop(0, STRIPES // BATCH)
    def _(group):
        for n in range(BATCH):
            k = group * BATCH + n
            done = acc[k, :HD, :] / acc[k, HD : HD + 1, :]
            for c in range(0, QPK, 2):
                two = [done[:, (c + d) * ROWS : (c + d + 1) * ROWS] for d in range(2)]
                att[k, :, c * HD : (c + 2) * HD] = jnp.concatenate(two, axis=0).T.astype(bf16)

    pltpu.make_async_copy(kv.at[pl.ds(0, GT)], pool, page_sem).wait()


def mix(att, w, out, got, acc, a_s, a_r):
    s, j = lax.axis_index("seq"), lax.axis_index("head")
    to = dealt(s, j)
    mine = to == s
    barrier = pltpu.get_barrier_semaphore()
    for r in range(8):
        h = lax.rem(j + r + 1, 8)
        if r < 7:
            pl.semaphore_signal(barrier, inc=1, device_id=(to, h), device_id_type=MESH)
        else:

            @pl.when(jnp.logical_not(mine))
            def _():
                pl.semaphore_signal(barrier, inc=1, device_id=(to, h), device_id_type=MESH)

    pl.semaphore_wait(barrier, jnp.where(mine, 7, 8))

    copies = []
    for r in range(STRIPES):
        k = lax.rem(s // 2 + j + r, STRIPES)
        own = mine & (s // 2 == k)
        cp = pltpu.make_async_remote_copy(
            src_ref=att.at[k],
            dst_ref=got.at[j],
            send_sem=a_s.at[k],
            recv_sem=a_r.at[j],
            device_id=held(s, k),
            device_id_type=MESH,
        )
        copies.append((own, cp))

        @pl.when(jnp.logical_not(own))
        def _():
            cp.start()

        @pl.when(own)
        def _():
            pltpu.make_async_copy(att.at[k], got.at[j], a_r.at[j]).start()

    for r in range(8):
        h = lax.rem(j + 8 - r, 8)
        pltpu.make_async_copy(got.at[h], got.at[h], a_r.at[h]).wait()
        part = jnp.dot(
            got[h], w[pl.ds(pl.multiple_of(h * QPK * HD, QPK * HD), QPK * HD), :], preferred_element_type=f32
        )
        if r == 0:
            acc[...] = part
        elif r < 7:
            acc[...] += part
        else:
            out[...] = (acc[...] + part).astype(bf16)
    for own, cp in copies:

        @pl.when(jnp.logical_not(own))
        def _():
            cp.wait_send()


ANY = pl.BlockSpec(memory_space=pl.ANY)
SMEM = pl.BlockSpec(memory_space=pltpu.SMEM)
VMEM = pl.BlockSpec(memory_space=pltpu.VMEM)
DMA = pltpu.SemaphoreType.DMA


HBM = pl.BlockSpec(memory_space=pltpu.HBM)


def projected(hidden, w_qkv, given):
    return pl.pallas_call(
        project,
        out_shape=(
            jax.ShapeDtypeStruct((STRIPES, ROWS, QPK * HD), bf16),
            jax.ShapeDtypeStruct((TOKENS, 2 * HD), bf16),
            jax.ShapeDtypeStruct((PAD + TOKENS, 2 * HD), bf16),
            jax.ShapeDtypeStruct((VR, PAD + TOKENS), bf16),
            jax.ShapeDtypeStruct((TOKENS // 128, 128), jnp.int32),
            jax.ShapeDtypeStruct((META, 128), jnp.int32),
        ),
        in_specs=[VMEM, HBM, VMEM],
        out_specs=(VMEM,) * 6,
        scratch_shapes=[
            pltpu.VMEM((KVH, D, 2 * HD), bf16),
            pltpu.VMEM((KVH, D, QPK * HD), bf16),
            pltpu.VMEM((KVH, ROWS, 2 * HD), bf16),
            pltpu.VMEM((KVH, ROWS, QPK * HD), bf16),
            DMA((16,)),
            DMA((7,)),
            DMA((7,)),
            DMA((8,)),
            DMA((8,)),
            DMA((15 * CHUNKS,)),
            DMA((15 * CHUNKS,)),
            DMA,
        ],
        compiler_params=pltpu.CompilerParams(collective_id=0, has_side_effects=True, vmem_limit_bytes=34 << 20),
        name="project",
    )(hidden, w_qkv, given)


def shards(hidden, w_qkv, w_out, seg_ids, live, page_table):
    pages = jnp.pad(page_table, (0, TOKENS - TOKENS // PAGE))
    given = (seg_ids + 16 * (1 - live) + 32 * pages).reshape(-1, 128)
    q, kv, kx, vt, code, meta = projected(hidden, w_qkv, given)
    att, pool = pl.pallas_call(
        attend,
        out_shape=(
            jax.ShapeDtypeStruct((STRIPES, ROWS, QPK * HD), bf16),
            jax.ShapeDtypeStruct((GT, 2 * HD), bf16),
        ),
        in_specs=[ANY, VMEM, VMEM, VMEM, VMEM, VMEM],
        out_specs=(VMEM, HBM),
        scratch_shapes=[
            pltpu.SMEM((META, 128), jnp.int32),
            pltpu.SMEM((ITEMS,), jnp.int32),
            pltpu.SMEM((ITEMS,), jnp.int32),
            pltpu.VMEM((STRIPES, 2 * HD, QPK * ROWS), bf16),
            pltpu.VMEM((STRIPES, 1, QPK * ROWS), f32),
            pltpu.VMEM((STRIPES, VR, QPK * ROWS), f32),
            pltpu.VMEM((BK, QPK * ROWS), f32),
            pltpu.VMEM((BK, QPK * ROWS), f32),
            DMA,
            DMA,
        ],
        compiler_params=pltpu.CompilerParams(vmem_limit_bytes=20 << 20),
        name="attend",
    )(meta, code, q, kv, kx, vt)

    mixed = pl.pallas_call(
        mix,
        out_shape=jax.ShapeDtypeStruct((ROWS, D), bf16),
        in_specs=[ANY, VMEM],
        out_specs=VMEM,
        scratch_shapes=[
            pltpu.VMEM((KVH, ROWS, QPK * HD), bf16),
            pltpu.VMEM((ROWS, D), f32),
            DMA((8,)),
            DMA((8,)),
        ],
        compiler_params=pltpu.CompilerParams(collective_id=1, has_side_effects=True, vmem_limit_bytes=12 << 20),
        name="mix",
    )(att, w_out)
    return mixed, pool.reshape(1, TOKENS // PAGE // SEQ, PAGE, 2 * HD)


def solution(mesh):
    placed = (P(("seq", "head"), None), P(), P(), P(), P(), P())
    return jax.shard_map(
        shards,
        mesh=mesh,
        in_specs=placed,
        out_specs=(P(("seq", "head"), None), P("head", "seq", None, None)),
        check_vma=False,
    )
```
